32 devices in a mesh: seq: 16 (over z, y, core), head: 2 (over x).
Axes of the slice: x: 2, y: 2, z: 4, core: 2. Of those that a mesh axis runs over, the one named last changes fastest.
Arguments:
- queries: bfloat16 [4096, 8192], P(('seq', 'head')), may hold values from -6 to 6
- keys: bfloat16 [4096, 8192], P(('seq', 'head')), may hold values from -6 to 6
- values: bfloat16 [4096, 8192], P(('seq', 'head')), may hold values from -70 to 70
- log_decay: float32 [64, 4096], P('head', 'seq'), may hold values from -1 to 0
- doc_lengths: int32 [32], replicated, may hold values from 1 to 1024, 4096 in all
- gain: float32 [8192], P('head'), may hold values from 0.25 to 1.75
Outputs:
- attended: bfloat16 [4096, 8192], P(('seq', 'head'))
The draws below stay inside these ranges and needn't reach their ends.
All inputs are finite; a program needn't handle non-finite values.
Results may differ from the reference program's by a relative error of at most 0.001.
Values may be sent and summed in bfloat16 or wider, within the bound.
A program may use at most 128 MiB of HBM per device.

```python
import functools
import math
import jax
import jax.numpy as jnp
import numpy as np
from jax import lax

HEAD_TOTAL = 64
DH = 128
TOK_DEV = 256
NDOC = 32
TOKEN_TOTAL = 4096


def draw_values(key, part):
    key_base, key_cols = jax.random.split(key, 2)
    column_scale = jnp.exp(jax.random.uniform(key_cols, (HEAD_TOTAL * DH,), jnp.float32, 0.0, math.log(10.0)))
    base = jnp.clip(jax.random.normal(key_base, (TOKEN_TOTAL, HEAD_TOTAL * DH), jnp.float32), -6.0, 6.0)
    return (base * column_scale[None, :]).astype(jnp.bfloat16)


def draw_log_decay(key, part):
    every_key = jax.random.split(key, 7)
    fast_share = 0.5
    fast = jax.random.uniform(every_key[0], (HEAD_TOTAL,), jnp.float32) < fast_share
    fast_rate = 1.0 / jax.random.uniform(every_key[1], (HEAD_TOTAL,), jnp.float32, 30.0, 50.0)
    slow_rate = jnp.exp(jax.random.uniform(every_key[2], (HEAD_TOTAL,), jnp.float32, math.log(0.05), math.log(0.2))) / TOKEN_TOTAL
    decay_rate = jnp.where(fast, fast_rate, slow_rate)
    per_token_decay = jnp.exp(jax.random.uniform(every_key[3], (HEAD_TOTAL, TOKEN_TOTAL), jnp.float32, -0.7, 0.7))
    segment_decay_factor = jnp.exp(jax.random.uniform(every_key[4], (HEAD_TOTAL, TOKEN_TOTAL // TOK_DEV), jnp.float32, -0.7, 0.7))
    segment_decay_factor = jnp.repeat(segment_decay_factor, TOK_DEV, axis=1)
    segment_offsets = jax.random.randint(every_key[5], (3,), 0, TOKEN_TOTAL)
    segment_length = jnp.log(jax.random.uniform(every_key[6], (3, HEAD_TOTAL), jnp.float32, 0.6, 0.8))
    token_positions = jnp.arange(TOKEN_TOTAL, dtype=jnp.int32)
    boundary_hits = (token_positions[None, :] == segment_offsets[:, None]).astype(jnp.float32)
    segment_count = jnp.sum(segment_length[:, :, None] * boundary_hits[:, None, :], axis=0)
    return -decay_rate[:, None] * per_token_decay * segment_decay_factor + segment_count


def levels(own_key, dims, cuts, low, top_value):
    def one(position, parts):
        steps = jax.random.uniform(jax.random.fold_in(jax.random.fold_in(own_key, 6), position), (parts,), jnp.float32, low / len(cuts), top_value / len(cuts))
        return jnp.repeat(jnp.exp(steps), dims[position] // parts).reshape((-1,) + (1,) * (len(dims) - position - 1))

    factor_of = one(*cuts[0])
    for cut in cuts[1:]:
        factor_of = factor_of * one(*cut)
    return factor_of


def split_up(amount, total, bound, lean):
    weights = [(1 << 20) // math.isqrt(standing ** lean) + 1 for standing in range(2, amount + 1)]
    rest, holding = total - bound - (amount - 1), [1] * (amount - 1)
    while rest > 0:
        candidates = [i for i in range(amount - 1) if holding[i] < bound]
        whole, left = sum([weights[i] for i in candidates]), rest
        for i in candidates:
            addition = min(bound - holding[i], max(1, left * weights[i] // whole), rest)
            holding[i] = holding[i] + addition
            rest = rest - addition
    return np.array([bound] + holding)


def ragged(stream_key, count, total, most, lean):
    if count == 2:
        one = jax.random.randint(stream_key, (), max(1, total - most), min(most, total - 1) + 1)
        return jnp.stack([one, total - one])
    lengths = jnp.asarray(split_up(count, total, most, lean), jnp.int32)
    couples = (count - 1) // 2
    source_of, receiver = lengths[1:1 + 2 * couples:2], lengths[2:2 + 2 * couples:2]
    margin = jnp.minimum(source_of - 1, most - receiver)
    passed = jax.random.randint(jax.random.fold_in(stream_key, 1), (couples,), 0, 1 << 20) % (margin + 1)
    lengths = lengths.at[1:1 + 2 * couples:2].set(source_of - passed).at[2:2 + 2 * couples:2].set(receiver + passed)
    return lengths[jax.random.permutation(jax.random.fold_in(stream_key, 2), count)]


def scatter_about(key, dims, scale, reach, cuts=(), held_as=jnp.bfloat16):
    values = scale * jax.random.normal(key, dims, jnp.float32)
    if cuts:
        values = values * levels(key, dims, cuts, -0.22, 0.18)
    return jnp.clip(values, -reach, reach).astype(held_as)


def setup_inputs(seed: int = 0) -> dict:
    seeds = jax.random.split(jax.random.key(seed), 7)
    return {
        "queries": scatter_about(seeds[0], (TOKEN_TOTAL, HEAD_TOTAL * DH), 1.0, 6.0, ((0, 32),)),
        "keys": scatter_about(seeds[1], (TOKEN_TOTAL, HEAD_TOTAL * DH), 1.0, 6.0, ((0, 32),)),
        "values": draw_values(jax.random.fold_in(seeds[6], 71), 0),
        "log_decay": draw_log_decay(jax.random.fold_in(seeds[6], 71), 0),
        "doc_lengths": ragged(seeds[4], NDOC, TOKEN_TOTAL, TOKEN_TOTAL // 4, 2).astype(jnp.int32),
        "gain": jnp.clip(1.0 + 0.15 * jax.random.normal(seeds[5], (HEAD_TOTAL * DH,), jnp.float32), 0.25, 1.75),
    }


HIGHEST = lax.Precision.HIGHEST

def block_step(gain_table, state, pieces):
    query_rows, key_rows, value_rows, decays, doc_block, previous = pieces
    query_rows = query_rows.astype(jnp.float32)
    key_rows = key_rows.astype(jnp.float32)
    value_rows = value_rows.astype(jnp.float32)
    decay_sum = jnp.cumsum(decays, axis=0)
    block_size = doc_block.shape[0]
    order_ids = jnp.arange(block_size, dtype=jnp.int32)
    allowed = (order_ids[:, None] >= order_ids[None, :]) & (doc_block[:, None] == doc_block[None, :])
    spread_mask = allowed[:, :, None]
    gaps = decay_sum[:, None, :] - decay_sum[None, :, :]
    weights = jnp.where(spread_mask, jnp.exp(jnp.where(spread_mask, gaps, 0.0)), 0.0)
    scores = jnp.einsum('ihd,jhd->ijh', query_rows, key_rows, precision=HIGHEST) * weights
    within = jnp.einsum('ijh,jhd->ihd', scores, value_rows, precision=HIGHEST)
    joined = (doc_block == previous).astype(decays.dtype)
    leading = jnp.exp(decay_sum) * joined[:, None]
    across = jnp.einsum('ihd,hde->ihe', query_rows * leading[:, :, None], state, precision=HIGHEST)
    tailing = jnp.exp(decay_sum[-1][None, :] - decay_sum) * (doc_block == doc_block[-1]).astype(decays.dtype)[:, None]
    local_state = jnp.einsum('jhd,jhe->hde', key_rows * tailing[:, :, None], value_rows, precision=HIGHEST)
    carried = jnp.exp(decay_sum[-1]) * (doc_block[-1] == previous).astype(decays.dtype)
    mixed = within + across
    mean_square = lax.optimization_barrier(jnp.mean(mixed * mixed, axis=-1, keepdims=True))
    normed = mixed * lax.rsqrt(mean_square + 1e-06) * gain_table[None, :, :]
    return (carried[:, None, None] * state + local_state, normed.astype(jnp.bfloat16))

def reference(queries, keys, values, log_decay, doc_lengths, gain):
    step_size = math.gcd(TOKEN_TOTAL, 128)
    blocks = TOKEN_TOTAL // step_size
    doc_ends = jnp.cumsum(doc_lengths).astype(jnp.int32)
    positions = jnp.arange(TOKEN_TOTAL, dtype=jnp.int32)
    doc_ids = lax.optimization_barrier(jnp.sum((doc_ends[None, :] <= positions[:, None]).astype(jnp.int32), axis=1)).astype(jnp.int32)
    doc_grid = doc_ids.reshape(blocks, step_size)
    previous = jnp.concatenate([jnp.full((1,), -1, jnp.int32), doc_grid[:-1, -1].astype(jnp.int32)])
    query_grid = queries.reshape(blocks, step_size, HEAD_TOTAL, DH)
    key_grid = keys.reshape(blocks, step_size, HEAD_TOTAL, DH)
    value_grid = values.reshape(blocks, step_size, HEAD_TOTAL, DH)
    decay_grid = log_decay.T.reshape(blocks, step_size, HEAD_TOTAL)
    initial = jnp.zeros((HEAD_TOTAL, DH, DH), jnp.float32)
    gain_table = gain.reshape(HEAD_TOTAL, DH)
    stepper = functools.partial(block_step, gain_table)
    final_state, outputs = lax.scan(stepper, initial, (query_grid, key_grid, value_grid, decay_grid, doc_grid, previous))
    return outputs.reshape(TOKEN_TOTAL, HEAD_TOTAL * DH)
```

```python
import functools

import jax
import jax.numpy as jnp
from jax import lax
from jax.experimental import pallas as pl
from jax.experimental.pallas import tpu as pltpu
from jax.sharding import PartitionSpec as P

HIGHEST = lax.Precision.HIGHEST


def prefix(part, axis, combine, identity):
    place = lax.axis_index(axis)
    gathered = jax.tree.map(lambda a: lax.all_gather(a, axis), part)
    state = jax.tree.map(lambda a, e: jnp.zeros_like(a) + jnp.asarray(e, a.dtype), part, identity)

    def one(turn, state):
        return combine(
            state, jax.tree.map(lambda a: lax.dynamic_index_in_dim(a, turn, 0, False), gathered)
        )

    return lax.fori_loop(0, place, one, state)


def link(earlier, later):
    factor_one, state_one = earlier
    factor_two, state_two = later
    return (factor_one * factor_two, factor_two[:, None, None] * state_one + state_two)


def make_identity(amount, head_width):
    return (
        jnp.ones((amount,), jnp.float32),
        jnp.zeros((amount, head_width, head_width), jnp.float32),
    )


def local(queries, keys, values, log_decay, doc_lengths, gain):
    query_rows, key_rows, value_rows = (
        lax.all_to_all(queries, "head", split_axis=1, concat_axis=0, tiled=True),
        lax.all_to_all(keys, "head", split_axis=1, concat_axis=0, tiled=True),
        lax.all_to_all(values, "head", split_axis=1, concat_axis=0, tiled=True),
    )
    head_count = log_decay.shape[0]
    row_count = key_rows.shape[0]
    head_width = key_rows.shape[1] // head_count
    doc_ends = jnp.cumsum(doc_lengths)
    first_row = lax.axis_index("seq") * row_count
    positions = first_row + jnp.arange(row_count, dtype=jnp.int32)
    doc_ids = jnp.sum((doc_ends[None, :] <= positions[:, None]).astype(jnp.int32), axis=1)
    prior_doc = jnp.sum((doc_ends <= first_row - 1).astype(jnp.int32))
    order_ids = jnp.arange(row_count, dtype=jnp.int32)
    allowed = (order_ids[:, None] >= order_ids[None, :]) & (doc_ids[:, None] == doc_ids[None, :])
    decay_sum = jnp.cumsum(log_decay, axis=1)
    tailing = (
        jnp.exp(decay_sum[:, -1:] - decay_sum)
        * (doc_ids == doc_ids[-1]).astype(jnp.float32)[None, :]
    )
    leading = jnp.exp(decay_sum) * (doc_ids == prior_doc).astype(jnp.float32)[None, :]
    carried = jnp.exp(decay_sum[:, -1]) * (doc_ids[-1] == prior_doc).astype(jnp.float32)
    head_ids = jnp.arange(head_count, dtype=jnp.int32)

    def pick(block, head_index):
        return lax.dynamic_slice_in_dim(block, head_index * head_width, head_width, 1)

    def own_state(head_index):
        weighted = pick(key_rows, head_index).astype(jnp.float32) * tailing[head_index][:, None]
        value_part = pick(value_rows, head_index).astype(jnp.float32)
        return jnp.einsum(
            "jd,je->de", weighted, value_part, precision=HIGHEST, preferred_element_type=jnp.float32
        )

    def within(head_index):
        scores = lax.dot_general(
            pick(query_rows, head_index),
            pick(key_rows, head_index),
            (((1,), (1,)), ((), ())),
            preferred_element_type=jnp.float32,
        )
        gaps = decay_sum[head_index][:, None] - decay_sum[head_index][None, :]
        weights = jnp.where(allowed, jnp.exp(jnp.where(allowed, gaps, 0.0)), 0.0)
        value_part = pick(value_rows, head_index).astype(jnp.float32)
        return jnp.dot(
            scores * weights, value_part, precision=HIGHEST, preferred_element_type=jnp.float32
        )

    def across(paired):
        head_index, state = paired
        scaled = pick(query_rows, head_index).astype(jnp.float32) * leading[head_index][:, None]
        return jnp.dot(scaled, state, precision=HIGHEST, preferred_element_type=jnp.float32)

    own = lax.map(own_state, head_ids)
    total_factor, incoming = prefix(
        (carried, own), "seq", link, make_identity(head_count, head_width)
    )
    far = lax.map(across, (head_ids, incoming))
    near = lax.map(within, head_ids)
    mixed = near + far
    mean_square = jnp.mean(mixed * mixed, axis=-1, keepdims=True)
    normed = mixed * lax.rsqrt(mean_square + 1e-06) * gain.reshape(head_count, 1, head_width)
    merged = (
        jnp.transpose(normed, (1, 0, 2))
        .reshape(row_count, head_count * head_width)
        .astype(jnp.bfloat16)
    )
    return lax.all_to_all(merged, "head", split_axis=0, concat_axis=1, tiled=True)


MESH = pl.DeviceIdType.MESH
GROUP = 8
SUBS = 2
TOP = 32766.0
FAR_BELOW = -1e30


def other(number, turn):
    out = 0
    for bit in (1, 2, 4):
        a, b = (number // bit) % 2, (turn // bit) % 2
        out = out + bit * (a + b - 2 * a * b)
    return out


def halves(x):
    high = x.astype(jnp.bfloat16)
    return high, (x - high.astype(jnp.float32)).astype(jnp.bfloat16)


def to_code(state):
    scale = jnp.maximum(jnp.max(jnp.abs(state), axis=0, keepdims=True), 1e-30) * (1.0 / TOP)
    code = jnp.round(state * (1.0 / scale)).astype(jnp.int32).astype(jnp.int16)
    return code, scale


def from_code(code):
    return code.astype(jnp.int32).astype(jnp.float32)


def slab_kernel(
    slabs,
    doc_ref, q_ref, k_ref, v_ref, ld_ref, gain_ref, o_ref,
    ld_all, gain_all, cum_t, bias, near,
    s_out, s_in, sm_out, sm_in, e_out, e_in, em_out, em_in, t_out, t_in,
    s_ss, s_rs, sm_ss, sm_rs, e_ss, e_rs, em_ss, em_rs, t_ss, t_rs, x_ss, x_rs,
):
    seq, half = lax.axis_index("seq"), lax.axis_index("head")
    block = seq * 2 + half
    slab, me = block // GROUP, block % GROUP
    rows, width = q_ref.shape[0], q_ref.shape[0]
    part = ld_ref.shape[0]
    count = 2 * part
    per_owner = count // GROUP
    per_sub = per_owner // SUBS

    def place(other_slab, number):
        b = other_slab * GROUP + number
        return (b // 2, b % 2)

    barrier = pltpu.get_barrier_semaphore()
    for turn in range(1, GROUP):
        pl.semaphore_signal(barrier, inc=1, device_id=place(slab, other(me, turn)), device_id_type=MESH)

    @pl.when(slab > 0)
    def _():
        pl.semaphore_signal(barrier, inc=1, device_id=place(slab - 1, me), device_id_type=MESH)

    @pl.when(slab < slabs - 1)
    def _():
        pl.semaphore_signal(barrier, inc=1, device_id=place(slab + 1, me), device_id_type=MESH)

    neighbours = GROUP - 1 + jnp.where(slab > 0, 1, 0) + jnp.where(slab < slabs - 1, 1, 0)
    pl.semaphore_wait(barrier, neighbours)

    mine = pl.ds(pl.multiple_of(half * part, part), part)
    swaps = [
        pltpu.make_async_remote_copy(
            src_ref=ld_ref.at[:, pl.ds(pl.multiple_of((1 - half) * rows, rows), rows)],
            dst_ref=ld_all.at[mine], send_sem=x_ss.at[0], recv_sem=x_rs.at[0],
            device_id=(seq, 1 - half), device_id_type=MESH),
        pltpu.make_async_remote_copy(
            src_ref=gain_ref, dst_ref=gain_all.at[mine], send_sem=x_ss.at[1], recv_sem=x_rs.at[1],
            device_id=(seq, 1 - half), device_id_type=MESH),
    ]
    for swap in swaps:
        swap.start()
    ld_all[mine, :] = ld_ref[:, pl.ds(pl.multiple_of(half * rows, rows), rows)]
    gain_all[mine, :] = gain_ref[...]

    first = block * rows
    down = lax.broadcasted_iota(jnp.int32, (rows, rows), 0)
    along = lax.broadcasted_iota(jnp.int32, (rows, rows), 1)
    doc_down = jnp.zeros((rows, rows), jnp.int32)
    doc_along = jnp.zeros((rows, rows), jnp.int32)
    prior = jnp.int32(0)
    final = jnp.int32(0)
    end = jnp.int32(0)
    for n in range(doc_ref.shape[0]):
        end = end + doc_ref[n]
        doc_down = doc_down + (down + first >= end).astype(jnp.int32)
        doc_along = doc_along + (along + first >= end).astype(jnp.int32)
        prior = prior + (end <= first - 1).astype(jnp.int32)
        final = final + (end <= first + rows - 1).astype(jnp.int32)
    bias[...] = jnp.where((down >= along) & (doc_down == doc_along), 0.0, FAR_BELOW)
    doc_few = doc_down[:, :per_owner]
    in_last = (doc_few == final).astype(jnp.float32)
    in_prior = (doc_few == prior).astype(jnp.float32)
    passes = (jnp.full((1, per_owner), final, jnp.int32) == prior).astype(jnp.float32)

    for swap in swaps:
        swap.wait()
    cum = jnp.dot(
        ld_all[...], (down <= along).astype(jnp.float32),
        precision=HIGHEST, preferred_element_type=jnp.float32,
    )
    turned = jnp.transpose(jnp.concatenate([cum, jnp.zeros((rows - count, rows), jnp.float32)], axis=0))
    for g in range(GROUP):
        cum_t[g] = turned[:, g * per_owner:(g + 1) * per_owner]

    def columns(g, c):
        return pl.ds(pl.multiple_of((g * per_owner + c) * width, width), width)

    def make_state(g, sub, code_ref, meta_ref):
        sums = cum_t[g]
        last = sums[rows - 1:rows, :]
        tail = jnp.exp(last - sums) * in_last
        carry = jnp.exp(last) * passes
        for i in range(per_sub):
            c = sub * per_sub + i
            cols = columns(g, c)
            high, low = halves(k_ref[:, cols].astype(jnp.float32) * tail[:, c:c + 1])
            value = v_ref[:, cols]
            state = lax.dot_general(
                jnp.concatenate([high, low], axis=0), jnp.concatenate([value, value], axis=0),
                (((0,), (0,)), ((), ())), preferred_element_type=jnp.float32,
            )
            code, scale = to_code(state)
            code_ref[i] = code
            meta_ref[i:i + 1, :] = scale
            meta_ref[per_sub + i:per_sub + i + 1, :] = jnp.broadcast_to(carry[:, c:c + 1], (1, width))

    def send_pair(sub, turn, out, into, ss, rs, m_out, m_in, m_ss, m_rs, slot, peer):
        to = place(slab, peer)
        return [
            pltpu.make_async_remote_copy(
                src_ref=m_out.at[sub, slot], dst_ref=m_in.at[sub, me], send_sem=m_ss.at[sub, turn],
                recv_sem=m_rs.at[sub, me], device_id=to, device_id_type=MESH),
            pltpu.make_async_remote_copy(
                src_ref=out.at[sub, slot], dst_ref=into.at[sub, me], send_sem=ss.at[sub, turn],
                recv_sem=rs.at[sub, me], device_id=to, device_id_type=MESH),
        ]

    def state_pair(sub, turn):
        return send_pair(sub, turn, s_out, s_in, s_ss, s_rs, sm_out, sm_in, sm_ss, sm_rs, turn, other(me, turn))

    def prefix_pair(sub, turn):
        peer = other(me, turn)
        return send_pair(sub, turn, e_out, e_in, e_ss, e_rs, em_out, em_in, em_ss, em_rs, peer, peer)

    def wait_arrival(sub, number, into, rs, m_in, m_rs):
        for ref, sem in ((m_in, m_rs), (into, rs)):
            pltpu.make_async_remote_copy(
                src_ref=ref.at[sub, number], dst_ref=ref.at[sub, number], send_sem=sem.at[sub, number],
                recv_sem=sem.at[sub, number], device_id=place(slab, number), device_id_type=MESH,
            ).wait_recv()

    def send_states(sub):
        @pl.loop(0, GROUP - 1)
        def _(step):
            turn = GROUP - 1 - step
            make_state(other(me, turn), sub, s_out.at[sub, turn], sm_out.at[sub, turn])
            for copy in state_pair(sub, turn):
                copy.start()

        make_state(me, sub, s_in.at[sub, me], sm_in.at[sub, me])

    def near_heads(low, high):
        @pl.loop(low, high)
        def _(g):
            sums = cum_t[g]
            for c in range(per_owner):
                cols = columns(g, c)
                scores = lax.dot_general(
                    q_ref[:, cols], k_ref[:, cols], (((1,), (1,)), ((), ())),
                    preferred_element_type=jnp.float32,
                )
                spread = jnp.broadcast_to(sums[:, c:c + 1], (rows, rows))
                flat = cum_rows[pl.ds(g * per_owner + c, 1), :]
                high_part, low_part = halves(scores * jnp.exp(spread - flat + bias[...]))
                value = v_ref[:, cols]
                near[:, cols] = jnp.dot(
                    jnp.concatenate([high_part, low_part], axis=1),
                    jnp.concatenate([value, value], axis=0),
                    preferred_element_type=jnp.float32,
                )

    def slab_totals(sub):
        @pl.loop(1, GROUP)
        def _(turn):
            wait_arrival(sub, other(me, turn), s_in, s_rs, sm_in, sm_rs)

        @pl.when(slab < slabs - 1)
        def _():
            @pl.loop(0, per_sub)
            def _(i):
                state = jnp.zeros((width, width), jnp.float32)
                for b in range(GROUP):
                    state = state * sm_in[sub, b, pl.ds(per_sub + i, 1), :] + from_code(s_in[sub, b, i]) * sm_in[
                        sub, b, pl.ds(i, 1), :]
                t_out[sub, i] = state

            total_copy(sub).start()

    def total_copy(sub):
        return pltpu.make_async_remote_copy(
            src_ref=t_out.at[sub], dst_ref=t_in.at[sub], send_sem=t_ss.at[sub], recv_sem=t_rs.at[sub],
            device_id=place(slab + 1, me), device_id_type=MESH)

    def send_prefixes(sub):
        @pl.when(slab > 0)
        def _():
            pltpu.make_async_remote_copy(
                src_ref=t_in.at[sub], dst_ref=t_in.at[sub], send_sem=t_ss.at[sub], recv_sem=t_rs.at[sub],
                device_id=place(slab - 1, me), device_id_type=MESH).wait_recv()

        @pl.when(slab == 0)
        def _():
            t_in[sub] = jnp.zeros(t_in.shape[1:], jnp.float32)

        @pl.loop(0, per_sub)
        def _(i):
            state = t_in[sub, i]
            for b in range(GROUP):
                code, scale = to_code(state)
                e_out[sub, b, i] = code
                em_out[sub, b, pl.ds(i, 1), :] = scale
                if b < GROUP - 1:
                    state = state * sm_in[sub, b, pl.ds(per_sub + i, 1), :] + from_code(s_in[sub, b, i]) * sm_in[
                        sub, b, pl.ds(i, 1), :]

        @pl.loop(0, GROUP - 1)
        def _(step):
            for copy in prefix_pair(sub, GROUP - 1 - step):
                copy.start()

    def finish(g, sub, codes, metas):
        sums = cum_t[g]
        lead = jnp.exp(sums) * in_prior
        for i in range(per_sub):
            c = sub * per_sub + i
            cols = columns(g, c)
            high, low = halves(from_code(codes[i]))
            query = q_ref[:, cols]
            far = jnp.dot(
                jnp.concatenate([query, query], axis=1), jnp.concatenate([high, low], axis=0),
                preferred_element_type=jnp.float32,
            )
            mixed = near[:, cols] + far * lead[:, c:c + 1] * metas[i:i + 1, :]
            square = jnp.mean(mixed * mixed, axis=1, keepdims=True)
            gains = gain_all[pl.ds(g * per_owner + c, 1), :]
            o_ref[:, cols] = (mixed * lax.rsqrt(square + 1e-06) * gains).astype(jnp.bfloat16)

    cum_rows = ld_all
    ld_all[...] = cum

    for sub in range(SUBS):
        send_states(sub)
    cuts = [0, GROUP // 2, 3 * GROUP // 4, GROUP]
    near_heads(cuts[0], cuts[1])
    slab_totals(0)
    near_heads(cuts[1], cuts[2])
    send_prefixes(0)
    slab_totals(1)
    near_heads(cuts[2], cuts[3])
    send_prefixes(1)
    for sub in range(SUBS):
        finish(me, sub, e_out.at[sub, me], em_out.at[sub, me])

        @pl.loop(1, GROUP)
        def _(turn, sub=sub):
            g = other(me, turn)
            wait_arrival(sub, g, e_in, e_rs, em_in, em_rs)
            finish(g, sub, e_in.at[sub, g], em_in.at[sub, g])

    for sub in range(SUBS):
        @pl.loop(1, GROUP)
        def _(turn, sub=sub):
            for copy in state_pair(sub, turn) + prefix_pair(sub, turn):
                copy.wait_send()

        @pl.when(slab < slabs - 1)
        def _(sub=sub):
            total_copy(sub).wait_send()


def by_slabs(slabs, queries, keys, values, log_decay, doc_lengths, gain):
    rows, columns = queries.shape
    part = log_decay.shape[0]
    count = 2 * part
    per_sub = count // GROUP // SUBS
    width = columns // count
    codes = pltpu.VMEM((SUBS, GROUP, per_sub, width, width), jnp.int16)
    metas = pltpu.VMEM((SUBS, GROUP, 2 * per_sub, width), jnp.float32)
    totals = pltpu.VMEM((SUBS, per_sub, width, width), jnp.float32)
    sems = pltpu.SemaphoreType.DMA
    vmem = pl.BlockSpec(memory_space=pltpu.VMEM)
    return pl.pallas_call(
        functools.partial(slab_kernel, slabs),
        out_shape=jax.ShapeDtypeStruct((rows, columns), jnp.bfloat16),
        in_specs=[pl.BlockSpec(memory_space=pltpu.SMEM)] + [vmem] * 5,
        out_specs=vmem,
        scratch_shapes=[
            pltpu.VMEM((count, rows), jnp.float32),
            pltpu.VMEM((count, width), jnp.float32),
            pltpu.VMEM((GROUP, rows, count // GROUP), jnp.float32),
            pltpu.VMEM((rows, rows), jnp.float32),
            pltpu.VMEM((rows, columns), jnp.float32),
            codes, codes, metas, metas, codes, codes, metas, metas, totals, totals,
        ] + [sems((SUBS, GROUP))] * 8 + [sems((SUBS,))] * 2 + [sems((2,))] * 2,
        compiler_params=pltpu.CompilerParams(
            collective_id=0, has_side_effects=True, vmem_limit_bytes=48 * 1024 * 1024
        ),
        cost_estimate=pl.CostEstimate(
            flops=14 * count * rows * rows * width, bytes_accessed=8 * rows * columns,
            transcendentals=count * rows * rows,
        ),
    )(doc_lengths, queries, keys, values, log_decay, gain.reshape(part, width))


def solution(mesh):
    devices = mesh.shape["seq"] * mesh.shape["head"]

    def run(queries, keys, values, log_decay, doc_lengths, gain):
        rows = queries.shape[0] // devices
        heads = log_decay.shape[0]
        width = queries.shape[1] // heads
        fits = (
            mesh.shape["head"] == 2 and devices % GROUP == 0 and rows == width == 128
            and GROUP * rows * 4 >= queries.shape[0] and heads % (GROUP * SUBS) == 0 and heads <= rows
        )
        body = functools.partial(by_slabs, devices // GROUP) if fits else local
        return jax.shard_map(
            body,
            mesh=mesh,
            in_specs=(
                P(("seq", "head"), None),
                P(("seq", "head"), None),
                P(("seq", "head"), None),
                P("head", "seq"),
                P(),
                P("head"),
            ),
            out_specs=P(("seq", "head"), None),
            check_vma=False,
        )(queries, keys, values, log_decay, doc_lengths, gain)

    return run
```

```python
import functools

import jax
import jax.numpy as jnp
from jax import lax
from jax.experimental import pallas as pl
from jax.experimental.pallas import tpu as pltpu
from jax.sharding import PartitionSpec as P

HIGHEST = lax.Precision.HIGHEST


def prefix(part, axis, combine, identity):
    place = lax.axis_index(axis)
    gathered = jax.tree.map(lambda a: lax.all_gather(a, axis), part)
    state = jax.tree.map(lambda a, e: jnp.zeros_like(a) + jnp.asarray(e, a.dtype), part, identity)

    def one(turn, state):
        return combine(
            state, jax.tree.map(lambda a: lax.dynamic_index_in_dim(a, turn, 0, False), gathered)
        )

    return lax.fori_loop(0, place, one, state)


def link(earlier, later):
    factor_one, state_one = earlier
    factor_two, state_two = later
    return (factor_one * factor_two, factor_two[:, None, None] * state_one + state_two)


def make_identity(amount, head_width):
    return (
        jnp.ones((amount,), jnp.float32),
        jnp.zeros((amount, head_width, head_width), jnp.float32),
    )


def local(queries, keys, values, log_decay, doc_lengths, gain):
    query_rows, key_rows, value_rows = (
        lax.all_to_all(queries, "head", split_axis=1, concat_axis=0, tiled=True),
        lax.all_to_all(keys, "head", split_axis=1, concat_axis=0, tiled=True),
        lax.all_to_all(values, "head", split_axis=1, concat_axis=0, tiled=True),
    )
    head_count = log_decay.shape[0]
    row_count = key_rows.shape[0]
    head_width = key_rows.shape[1] // head_count
    doc_ends = jnp.cumsum(doc_lengths)
    first_row = lax.axis_index("seq") * row_count
    positions = first_row + jnp.arange(row_count, dtype=jnp.int32)
    doc_ids = jnp.sum((doc_ends[None, :] <= positions[:, None]).astype(jnp.int32), axis=1)
    prior_doc = jnp.sum((doc_ends <= first_row - 1).astype(jnp.int32))
    order_ids = jnp.arange(row_count, dtype=jnp.int32)
    allowed = (order_ids[:, None] >= order_ids[None, :]) & (doc_ids[:, None] == doc_ids[None, :])
    decay_sum = jnp.cumsum(log_decay, axis=1)
    tailing = (
        jnp.exp(decay_sum[:, -1:] - decay_sum)
        * (doc_ids == doc_ids[-1]).astype(jnp.float32)[None, :]
    )
    leading = jnp.exp(decay_sum) * (doc_ids == prior_doc).astype(jnp.float32)[None, :]
    carried = jnp.exp(decay_sum[:, -1]) * (doc_ids[-1] == prior_doc).astype(jnp.float32)
    head_ids = jnp.arange(head_count, dtype=jnp.int32)

    def pick(block, head_index):
        return lax.dynamic_slice_in_dim(block, head_index * head_width, head_width, 1)

    def own_state(head_index):
        weighted = pick(key_rows, head_index).astype(jnp.float32) * tailing[head_index][:, None]
        value_part = pick(value_rows, head_index).astype(jnp.float32)
        return jnp.einsum(
            "jd,je->de", weighted, value_part, precision=HIGHEST, preferred_element_type=jnp.float32
        )

    def within(head_index):
        scores = lax.dot_general(
            pick(query_rows, head_index),
            pick(key_rows, head_index),
            (((1,), (1,)), ((), ())),
            preferred_element_type=jnp.float32,
        )
        gaps = decay_sum[head_index][:, None] - decay_sum[head_index][None, :]
        weights = jnp.where(allowed, jnp.exp(jnp.where(allowed, gaps, 0.0)), 0.0)
        value_part = pick(value_rows, head_index).astype(jnp.float32)
        return jnp.dot(
            scores * weights, value_part, precision=HIGHEST, preferred_element_type=jnp.float32
        )

    def across(paired):
        head_index, state = paired
        scaled = pick(query_rows, head_index).astype(jnp.float32) * leading[head_index][:, None]
        return jnp.dot(scaled, state, precision=HIGHEST, preferred_element_type=jnp.float32)

    own = lax.map(own_state, head_ids)
    total_factor, incoming = prefix(
        (carried, own), "seq", link, make_identity(head_count, head_width)
    )
    far = lax.map(across, (head_ids, incoming))
    near = lax.map(within, head_ids)
    mixed = near + far
    mean_square = jnp.mean(mixed * mixed, axis=-1, keepdims=True)
    normed = mixed * lax.rsqrt(mean_square + 1e-06) * gain.reshape(head_count, 1, head_width)
    merged = (
        jnp.transpose(normed, (1, 0, 2))
        .reshape(row_count, head_count * head_width)
        .astype(jnp.bfloat16)
    )
    return lax.all_to_all(merged, "head", split_axis=0, concat_axis=1, tiled=True)


MESH = pl.DeviceIdType.MESH
GROUP = 8
SUBS = 2
TOP = 32766.0
FAR_BELOW = -1e30
ORDER = (7, 6, 1, 5, 4, 3, 2)


def other(number, turn):
    out = 0
    for bit in (1, 2, 4):
        a, b = (number // bit) % 2, (turn // bit) % 2
        out = out + bit * (a + b - 2 * a * b)
    return out


def turn_at(step):
    out = 0
    for i, turn in enumerate(ORDER):
        out = out + jnp.where(step == i, turn, 0)
    return out


def halves(x):
    high = x.astype(jnp.bfloat16)
    return high, (x - high.astype(jnp.float32)).astype(jnp.bfloat16)


def to_code(state):
    scale = jnp.maximum(jnp.max(jnp.abs(state), axis=0, keepdims=True), 1e-30) * (1.0 / TOP)
    code = jnp.round(state * (1.0 / scale)).astype(jnp.int32).astype(jnp.int16)
    return code, scale


def from_code(code):
    return code.astype(jnp.int32).astype(jnp.float32)


def slab_kernel(
    slabs,
    doc_ref, q_far, k_far, v_far, ld_ref, gain_ref, o_ref,
    q_ref, k_ref, v_ref,
    ld_all, gain_all, cum_t, bias, near,
    s_out, s_in, sm_out, sm_in, e_out, e_in, em_out, em_in, t_out, t_in,
    s_ss, s_rs, sm_ss, sm_rs, e_ss, e_rs, em_ss, em_rs, t_ss, t_rs, x_ss, x_rs, l_s,
):
    seq, half = lax.axis_index("seq"), lax.axis_index("head")
    block = seq * 2 + half
    slab, me = block // GROUP, block % GROUP
    rows, width = q_ref.shape[0], q_ref.shape[0]
    part = ld_ref.shape[0]
    count = 2 * part
    per_owner = count // GROUP
    per_sub = per_owner // SUBS

    def place(other_slab, number):
        b = other_slab * GROUP + number
        return (b // 2, b % 2)

    loads = [
        pltpu.make_async_copy(far_ref, near_ref, l_s.at[i])
        for i, (far_ref, near_ref) in enumerate(((k_far, k_ref), (v_far, v_ref), (q_far, q_ref)))
    ]
    for load in loads:
        load.start()

    barrier = pltpu.get_barrier_semaphore()
    for turn in range(1, GROUP):
        pl.semaphore_signal(barrier, inc=1, device_id=place(slab, other(me, turn)), device_id_type=MESH)

    @pl.when(slab > 0)
    def _():
        pl.semaphore_signal(barrier, inc=1, device_id=place(slab - 1, me), device_id_type=MESH)

    @pl.when(slab < slabs - 1)
    def _():
        pl.semaphore_signal(barrier, inc=1, device_id=place(slab + 1, me), device_id_type=MESH)

    neighbours = GROUP - 1 + jnp.where(slab > 0, 1, 0) + jnp.where(slab < slabs - 1, 1, 0)
    pl.semaphore_wait(barrier, neighbours)

    mine = pl.ds(pl.multiple_of(half * part, part), part)
    swaps = [
        pltpu.make_async_remote_copy(
            src_ref=ld_ref.at[:, pl.ds(pl.multiple_of((1 - half) * rows, rows), rows)],
            dst_ref=ld_all.at[mine], send_sem=x_ss.at[0], recv_sem=x_rs.at[0],
            device_id=(seq, 1 - half), device_id_type=MESH),
        pltpu.make_async_remote_copy(
            src_ref=gain_ref, dst_ref=gain_all.at[mine], send_sem=x_ss.at[1], recv_sem=x_rs.at[1],
            device_id=(seq, 1 - half), device_id_type=MESH),
    ]
    for swap in swaps:
        swap.start()
    ld_all[mine, :] = ld_ref[:, pl.ds(pl.multiple_of(half * rows, rows), rows)]
    gain_all[mine, :] = gain_ref[...]

    first = block * rows
    down = lax.broadcasted_iota(jnp.int32, (rows, rows), 0)
    along = lax.broadcasted_iota(jnp.int32, (rows, rows), 1)
    doc_down = jnp.zeros((rows, rows), jnp.int32)
    doc_along = jnp.zeros((rows, rows), jnp.int32)
    prior = jnp.int32(0)
    final = jnp.int32(0)
    end = jnp.int32(0)
    for n in range(doc_ref.shape[0]):
        end = end + doc_ref[n]
        doc_down = doc_down + (down + first >= end).astype(jnp.int32)
        doc_along = doc_along + (along + first >= end).astype(jnp.int32)
        prior = prior + (end <= first - 1).astype(jnp.int32)
        final = final + (end <= first + rows - 1).astype(jnp.int32)
    bias[...] = jnp.where((down >= along) & (doc_down == doc_along), 0.0, FAR_BELOW)
    doc_few = doc_down[:, :per_owner]
    in_last = (doc_few == final).astype(jnp.float32)
    in_prior = (doc_few == prior).astype(jnp.float32)
    passes = (jnp.full((1, per_owner), final, jnp.int32) == prior).astype(jnp.float32)

    for swap in swaps:
        swap.wait()
    cum = jnp.dot(
        ld_all[...], (down <= along).astype(jnp.float32),
        precision=HIGHEST, preferred_element_type=jnp.float32,
    )
    turned = jnp.transpose(jnp.concatenate([cum, jnp.zeros((rows - count, rows), jnp.float32)], axis=0))
    for g in range(GROUP):
        cum_t[g] = turned[:, g * per_owner:(g + 1) * per_owner]

    def columns(g, c):
        return pl.ds(pl.multiple_of((g * per_owner + c) * width, width), width)

    def make_state(g, sub, code_ref, meta_ref):
        sums = cum_t[g]
        last = sums[rows - 1:rows, :]
        tail = jnp.exp(last - sums) * in_last
        carry = jnp.exp(last) * passes
        for i in range(per_sub):
            c = sub * per_sub + i
            cols = columns(g, c)
            high, low = halves(v_ref[:, cols].astype(jnp.float32) * tail[:, c:c + 1])
            key = jnp.transpose(k_ref[:, cols])
            state = jnp.dot(
                jnp.concatenate([key, key], axis=1), jnp.concatenate([high, low], axis=0),
                preferred_element_type=jnp.float32,
            )
            code, scale = to_code(state)
            code_ref[i] = code
            meta_ref[i:i + 1, :] = scale
            meta_ref[per_sub + i:per_sub + i + 1, :] = jnp.broadcast_to(carry[:, c:c + 1], (1, width))

    def send_pair(sub, turn, out, into, ss, rs, m_out, m_in, m_ss, m_rs, slot, peer):
        to = place(slab, peer)
        return [
            pltpu.make_async_remote_copy(
                src_ref=m_out.at[sub, slot], dst_ref=m_in.at[sub, me], send_sem=m_ss.at[sub, turn],
                recv_sem=m_rs.at[sub, me], device_id=to, device_id_type=MESH),
            pltpu.make_async_remote_copy(
                src_ref=out.at[sub, slot], dst_ref=into.at[sub, me], send_sem=ss.at[sub, turn],
                recv_sem=rs.at[sub, me], device_id=to, device_id_type=MESH),
        ]

    def state_pair(sub, turn):
        return send_pair(sub, turn, s_out, s_in, s_ss, s_rs, sm_out, sm_in, sm_ss, sm_rs, turn, other(me, turn))

    def prefix_pair(sub, turn):
        peer = other(me, turn)
        return send_pair(sub, turn, e_out, e_in, e_ss, e_rs, em_out, em_in, em_ss, em_rs, peer, peer)

    def wait_arrival(sub, number, into, rs, m_in, m_rs):
        for ref, sem in ((m_in, m_rs), (into, rs)):
            pltpu.make_async_remote_copy(
                src_ref=ref.at[sub, number], dst_ref=ref.at[sub, number], send_sem=sem.at[sub, number],
                recv_sem=sem.at[sub, number], device_id=place(slab, number), device_id_type=MESH,
            ).wait_recv()

    def send_states(sub):
        @pl.loop(0, GROUP - 1)
        def _(step):
            turn = turn_at(step)
            make_state(other(me, turn), sub, s_out.at[sub, turn], sm_out.at[sub, turn])
            for copy in state_pair(sub, turn):
                copy.start()

        make_state(me, sub, s_in.at[sub, me], sm_in.at[sub, me])

    def near_heads(low, high):
        @pl.loop(low, high)
        def _(g):
            sums = cum_t[g]
            for c in range(per_owner):
                cols = columns(g, c)
                scores = lax.dot_general(
                    q_ref[:, cols], k_ref[:, cols], (((1,), (1,)), ((), ())),
                    preferred_element_type=jnp.float32,
                )
                spread = jnp.broadcast_to(sums[:, c:c + 1], (rows, rows))
                flat = cum_rows[pl.ds(g * per_owner + c, 1), :]
                high_part, low_part = halves(scores * jnp.exp(spread - flat + bias[...]))
                value = v_ref[:, cols]
                near[:, cols] = jnp.dot(
                    jnp.concatenate([high_part, low_part], axis=1),
                    jnp.concatenate([value, value], axis=0),
                    preferred_element_type=jnp.float32,
                )

    def slab_totals(sub):
        @pl.loop(1, GROUP)
        def _(turn):
            wait_arrival(sub, other(me, turn), s_in, s_rs, sm_in, sm_rs)

        @pl.when(slab < slabs - 1)
        def _():
            @pl.loop(0, per_sub)
            def _(i):
                state = jnp.zeros((width, width), jnp.float32)
                for b in range(GROUP):
                    state = state * sm_in[sub, b, pl.ds(per_sub + i, 1), :] + from_code(s_in[sub, b, i]) * sm_in[
                        sub, b, pl.ds(i, 1), :]
                t_out[sub, i] = state

            total_copy(sub).start()

    def total_copy(sub):
        return pltpu.make_async_remote_copy(
            src_ref=t_out.at[sub], dst_ref=t_in.at[sub], send_sem=t_ss.at[sub], recv_sem=t_rs.at[sub],
            device_id=place(slab + 1, me), device_id_type=MESH)

    def send_prefixes(sub):
        @pl.when(slab > 0)
        def _():
            pltpu.make_async_remote_copy(
                src_ref=t_in.at[sub], dst_ref=t_in.at[sub], send_sem=t_ss.at[sub], recv_sem=t_rs.at[sub],
                device_id=place(slab - 1, me), device_id_type=MESH).wait_recv()

        @pl.when(slab == 0)
        def _():
            t_in[sub] = jnp.zeros(t_in.shape[1:], jnp.float32)

        @pl.loop(0, per_sub)
        def _(i):
            state = t_in[sub, i]
            for b in range(GROUP):
                code, scale = to_code(state)
                e_out[sub, b, i] = code
                em_out[sub, b, pl.ds(i, 1), :] = scale
                if b < GROUP - 1:
                    state = state * sm_in[sub, b, pl.ds(per_sub + i, 1), :] + from_code(s_in[sub, b, i]) * sm_in[
                        sub, b, pl.ds(i, 1), :]

        @pl.loop(0, GROUP - 1)
        def _(step):
            for copy in prefix_pair(sub, turn_at(step)):
                copy.start()

    def finish(g, sub, codes, metas):
        sums = cum_t[g]
        lead = jnp.exp(sums) * in_prior
        for i in range(per_sub):
            c = sub * per_sub + i
            cols = columns(g, c)
            high, low = halves(from_code(codes[i]))
            query = q_ref[:, cols]
            far = jnp.dot(
                jnp.concatenate([query, query], axis=1), jnp.concatenate([high, low], axis=0),
                preferred_element_type=jnp.float32,
            )
            mixed = near[:, cols] + far * lead[:, c:c + 1] * metas[i:i + 1, :]
            square = jnp.mean(mixed * mixed, axis=1, keepdims=True)
            gains = gain_all[pl.ds(g * per_owner + c, 1), :]
            o_ref[:, cols] = (mixed * lax.rsqrt(square + 1e-06) * gains).astype(jnp.bfloat16)

    cum_rows = ld_all
    ld_all[...] = cum

    loads[0].wait()
    loads[1].wait()
    for sub in range(SUBS):
        send_states(sub)
    loads[2].wait()
    slab_totals(0)
    near_heads(0, 1)
    send_prefixes(0)
    near_heads(1, 3)
    slab_totals(1)
    near_heads(3, 4)
    send_prefixes(1)
    near_heads(4, GROUP)
    for sub in range(SUBS):
        finish(me, sub, e_out.at[sub, me], em_out.at[sub, me])

        @pl.loop(0, GROUP - 1)
        def _(step, sub=sub):
            g = other(me, turn_at(step))
            wait_arrival(sub, g, e_in, e_rs, em_in, em_rs)
            finish(g, sub, e_in.at[sub, g], em_in.at[sub, g])

    for sub in range(SUBS):
        @pl.loop(1, GROUP)
        def _(turn, sub=sub):
            for copy in state_pair(sub, turn) + prefix_pair(sub, turn):
                copy.wait_send()

        @pl.when(slab < slabs - 1)
        def _(sub=sub):
            total_copy(sub).wait_send()


def by_slabs(slabs, queries, keys, values, log_decay, doc_lengths, gain):
    rows, columns = queries.shape
    part = log_decay.shape[0]
    count = 2 * part
    per_sub = count // GROUP // SUBS
    width = columns // count
    codes = pltpu.VMEM((SUBS, GROUP, per_sub, width, width), jnp.int16)
    metas = pltpu.VMEM((SUBS, GROUP, 2 * per_sub, width), jnp.float32)
    totals = pltpu.VMEM((SUBS, per_sub, width, width), jnp.float32)
    sems = pltpu.SemaphoreType.DMA
    vmem = pl.BlockSpec(memory_space=pltpu.VMEM)
    return pl.pallas_call(
        functools.partial(slab_kernel, slabs),
        out_shape=jax.ShapeDtypeStruct((rows, columns), jnp.bfloat16),
        in_specs=[pl.BlockSpec(memory_space=pltpu.SMEM)] + [pl.BlockSpec(memory_space=pltpu.HBM)] * 3 + [vmem] * 2,
        out_specs=vmem,
        scratch_shapes=[pltpu.VMEM((rows, columns), jnp.bfloat16)] * 3 + [
            pltpu.VMEM((count, rows), jnp.float32),
            pltpu.VMEM((count, width), jnp.float32),
            pltpu.VMEM((GROUP, rows, count // GROUP), jnp.float32),
            pltpu.VMEM((rows, rows), jnp.float32),
            pltpu.VMEM((rows, columns), jnp.float32),
            codes, codes, metas, metas, codes, codes, metas, metas, totals, totals,
        ] + [sems((SUBS, GROUP))] * 8 + [sems((SUBS,))] * 2 + [sems((2,))] * 2 + [sems((3,))],
        compiler_params=pltpu.CompilerParams(
            collective_id=0, has_side_effects=True, vmem_limit_bytes=56 * 1024 * 1024
        ),
        cost_estimate=pl.CostEstimate(
            flops=14 * count * rows * rows * width, bytes_accessed=8 * rows * columns,
            transcendentals=count * rows * rows,
        ),
    )(doc_lengths, queries, keys, values, log_decay, gain.reshape(part, width))


def solution(mesh):
    devices = mesh.shape["seq"] * mesh.shape["head"]

    def run(queries, keys, values, log_decay, doc_lengths, gain):
        rows = queries.shape[0] // devices
        heads = log_decay.shape[0]
        width = queries.shape[1] // heads
        fits = (
            mesh.shape["head"] == 2 and devices % GROUP == 0 and rows == width == 128
            and GROUP * rows * 4 >= queries.shape[0] and heads % (GROUP * SUBS) == 0 and heads <= rows
        )
        body = functools.partial(by_slabs, devices // GROUP) if fits else local
        return jax.shard_map(
            body,
            mesh=mesh,
            in_specs=(
                P(("seq", "head"), None),
                P(("seq", "head"), None),
                P(("seq", "head"), None),
                P("head", "seq"),
                P(),
                P("head"),
            ),
            out_specs=P(("seq", "head"), None),
            check_vma=False,
        )(queries, keys, values, log_decay, doc_lengths, gain)

    return run
```

```python
import functools

import jax
import jax.numpy as jnp
from jax import lax
from jax.experimental import pallas as pl
from jax.experimental.pallas import tpu as pltpu
from jax.sharding import PartitionSpec as P

HIGHEST = lax.Precision.HIGHEST


def prefix(part, axis, combine, identity):
    place = lax.axis_index(axis)
    gathered = jax.tree.map(lambda a: lax.all_gather(a, axis), part)
    state = jax.tree.map(lambda a, e: jnp.zeros_like(a) + jnp.asarray(e, a.dtype), part, identity)

    def one(turn, state):
        return combine(
            state, jax.tree.map(lambda a: lax.dynamic_index_in_dim(a, turn, 0, False), gathered)
        )

    return lax.fori_loop(0, place, one, state)


def link(earlier, later):
    factor_one, state_one = earlier
    factor_two, state_two = later
    return (factor_one * factor_two, factor_two[:, None, None] * state_one + state_two)


def make_identity(amount, head_width):
    return (
        jnp.ones((amount,), jnp.float32),
        jnp.zeros((amount, head_width, head_width), jnp.float32),
    )


def local(queries, keys, values, log_decay, doc_lengths, gain):
    query_rows, key_rows, value_rows = (
        lax.all_to_all(queries, "head", split_axis=1, concat_axis=0, tiled=True),
        lax.all_to_all(keys, "head", split_axis=1, concat_axis=0, tiled=True),
        lax.all_to_all(values, "head", split_axis=1, concat_axis=0, tiled=True),
    )
    head_count = log_decay.shape[0]
    row_count = key_rows.shape[0]
    head_width = key_rows.shape[1] // head_count
    doc_ends = jnp.cumsum(doc_lengths)
    first_row = lax.axis_index("seq") * row_count
    positions = first_row + jnp.arange(row_count, dtype=jnp.int32)
    doc_ids = jnp.sum((doc_ends[None, :] <= positions[:, None]).astype(jnp.int32), axis=1)
    prior_doc = jnp.sum((doc_ends <= first_row - 1).astype(jnp.int32))
    order_ids = jnp.arange(row_count, dtype=jnp.int32)
    allowed = (order_ids[:, None] >= order_ids[None, :]) & (doc_ids[:, None] == doc_ids[None, :])
    decay_sum = jnp.cumsum(log_decay, axis=1)
    tailing = (
        jnp.exp(decay_sum[:, -1:] - decay_sum)
        * (doc_ids == doc_ids[-1]).astype(jnp.float32)[None, :]
    )
    leading = jnp.exp(decay_sum) * (doc_ids == prior_doc).astype(jnp.float32)[None, :]
    carried = jnp.exp(decay_sum[:, -1]) * (doc_ids[-1] == prior_doc).astype(jnp.float32)
    head_ids = jnp.arange(head_count, dtype=jnp.int32)

    def pick(block, head_index):
        return lax.dynamic_slice_in_dim(block, head_index * head_width, head_width, 1)

    def own_state(head_index):
        weighted = pick(key_rows, head_index).astype(jnp.float32) * tailing[head_index][:, None]
        value_part = pick(value_rows, head_index).astype(jnp.float32)
        return jnp.einsum(
            "jd,je->de", weighted, value_part, precision=HIGHEST, preferred_element_type=jnp.float32
        )

    def within(head_index):
        scores = lax.dot_general(
            pick(query_rows, head_index),
            pick(key_rows, head_index),
            (((1,), (1,)), ((), ())),
            preferred_element_type=jnp.float32,
        )
        gaps = decay_sum[head_index][:, None] - decay_sum[head_index][None, :]
        weights = jnp.where(allowed, jnp.exp(jnp.where(allowed, gaps, 0.0)), 0.0)
        value_part = pick(value_rows, head_index).astype(jnp.float32)
        return jnp.dot(
            scores * weights, value_part, precision=HIGHEST, preferred_element_type=jnp.float32
        )

    def across(paired):
        head_index, state = paired
        scaled = pick(query_rows, head_index).astype(jnp.float32) * leading[head_index][:, None]
        return jnp.dot(scaled, state, precision=HIGHEST, preferred_element_type=jnp.float32)

    own = lax.map(own_state, head_ids)
    total_factor, incoming = prefix(
        (carried, own), "seq", link, make_identity(head_count, head_width)
    )
    far = lax.map(across, (head_ids, incoming))
    near = lax.map(within, head_ids)
    mixed = near + far
    mean_square = jnp.mean(mixed * mixed, axis=-1, keepdims=True)
    normed = mixed * lax.rsqrt(mean_square + 1e-06) * gain.reshape(head_count, 1, head_width)
    merged = (
        jnp.transpose(normed, (1, 0, 2))
        .reshape(row_count, head_count * head_width)
        .astype(jnp.bfloat16)
    )
    return lax.all_to_all(merged, "head", split_axis=0, concat_axis=1, tiled=True)


MESH = pl.DeviceIdType.MESH
GROUP = 8
SUBS = 2
BATCH = 4
TOP = 32766.0
FAR_BELOW = -1e30
ORDER = (7, 6, 1, 5, 4, 3, 2)


def other(number, turn):
    out = 0
    for bit in (1, 2, 4):
        a, b = (number // bit) % 2, (turn // bit) % 2
        out = out + bit * (a + b - 2 * a * b)
    return out


def turn_at(step):
    out = 0
    for i, turn in enumerate(ORDER):
        out = out + jnp.where(step == i, turn, 0)
    return out


def halves(x):
    high = x.astype(jnp.bfloat16)
    return high, (x - high.astype(jnp.float32)).astype(jnp.bfloat16)


def to_code(state):
    scale = jnp.maximum(jnp.max(jnp.abs(state), axis=0, keepdims=True), 1e-30) * (1.0 / TOP)
    code = jnp.round(state * (1.0 / scale)).astype(jnp.int32).astype(jnp.int16)
    return code, scale


def from_code(code):
    return code.astype(jnp.int32).astype(jnp.float32)


def slab_kernel(
    slabs,
    doc_ref, q_far, k_far, v_far, ld_ref, gain_ref, o_ref,
    q_ref, k_ref, v_ref,
    ld_all, gain_all, cum_t, bias, near,
    s_out, s_in, sm_out, sm_in, e_out, e_in, em_out, em_in, t_out, t_in,
    s_ss, s_rs, sm_ss, sm_rs, e_ss, e_rs, em_ss, em_rs, t_ss, t_rs, x_ss, x_rs, l_s,
):
    seq, half = lax.axis_index("seq"), lax.axis_index("head")
    block = seq * 2 + half
    slab, me = block // GROUP, block % GROUP
    rows, width = q_ref.shape[0], q_ref.shape[0]
    part = ld_ref.shape[0]
    count = 2 * part
    per_owner = count // GROUP
    per_sub = per_owner // SUBS

    def place(other_slab, number):
        b = other_slab * GROUP + number
        return (b // 2, b % 2)

    loads = [
        pltpu.make_async_copy(far_ref, near_ref, l_s.at[i])
        for i, (far_ref, near_ref) in enumerate(((k_far, k_ref), (v_far, v_ref), (q_far, q_ref)))
    ]
    for load in loads:
        load.start()

    barrier = pltpu.get_barrier_semaphore()
    for turn in range(1, GROUP):
        pl.semaphore_signal(barrier, inc=1, device_id=place(slab, other(me, turn)), device_id_type=MESH)

    @pl.when(slab > 0)
    def _():
        pl.semaphore_signal(barrier, inc=1, device_id=place(slab - 1, me), device_id_type=MESH)

    @pl.when(slab < slabs - 1)
    def _():
        pl.semaphore_signal(barrier, inc=1, device_id=place(slab + 1, me), device_id_type=MESH)

    neighbours = GROUP - 1 + jnp.where(slab > 0, 1, 0) + jnp.where(slab < slabs - 1, 1, 0)
    pl.semaphore_wait(barrier, neighbours)

    mine = pl.ds(pl.multiple_of(half * part, part), part)
    swaps = [
        pltpu.make_async_remote_copy(
            src_ref=ld_ref.at[:, pl.ds(pl.multiple_of((1 - half) * rows, rows), rows)],
            dst_ref=ld_all.at[mine], send_sem=x_ss.at[0], recv_sem=x_rs.at[0],
            device_id=(seq, 1 - half), device_id_type=MESH),
        pltpu.make_async_remote_copy(
            src_ref=gain_ref, dst_ref=gain_all.at[mine], send_sem=x_ss.at[1], recv_sem=x_rs.at[1],
            device_id=(seq, 1 - half), device_id_type=MESH),
    ]
    for swap in swaps:
        swap.start()
    ld_all[mine, :] = ld_ref[:, pl.ds(pl.multiple_of(half * rows, rows), rows)]
    gain_all[mine, :] = gain_ref[...]

    first = block * rows
    down = lax.broadcasted_iota(jnp.int32, (rows, rows), 0)
    along = lax.broadcasted_iota(jnp.int32, (rows, rows), 1)
    doc_down = jnp.zeros((rows, rows), jnp.int32)
    doc_along = jnp.zeros((rows, rows), jnp.int32)
    prior = jnp.int32(0)
    final = jnp.int32(0)
    end = jnp.int32(0)
    for n in range(doc_ref.shape[0]):
        end = end + doc_ref[n]
        doc_down = doc_down + (down + first >= end).astype(jnp.int32)
        doc_along = doc_along + (along + first >= end).astype(jnp.int32)
        prior = prior + (end <= first - 1).astype(jnp.int32)
        final = final + (end <= first + rows - 1).astype(jnp.int32)
    bias[...] = jnp.where((down >= along) & (doc_down == doc_along), 0.0, FAR_BELOW)
    doc_few = doc_down[:, :per_owner]
    in_last = (doc_few == final).astype(jnp.float32)
    in_prior = (doc_few == prior).astype(jnp.float32)
    passes = (jnp.full((1, per_owner), final, jnp.int32) == prior).astype(jnp.float32)

    for swap in swaps:
        swap.wait()
    cum = jnp.dot(
        ld_all[...], (down <= along).astype(jnp.float32),
        precision=HIGHEST, preferred_element_type=jnp.float32,
    )
    turned = jnp.transpose(jnp.concatenate([cum, jnp.zeros((rows - count, rows), jnp.float32)], axis=0))
    for g in range(GROUP):
        cum_t[g] = turned[:, g * per_owner:(g + 1) * per_owner]

    def columns(g, c):
        return pl.ds(pl.multiple_of((g * per_owner + c) * width, width), width)

    def make_state(g, sub, code_ref, meta_ref):
        sums = cum_t[g]
        last = sums[rows - 1:rows, :]
        tail = jnp.exp(last - sums) * in_last
        carry = jnp.exp(last) * passes
        states = []
        for i in range(per_sub):
            c = sub * per_sub + i
            cols = columns(g, c)
            high, low = halves(v_ref[:, cols].astype(jnp.float32) * tail[:, c:c + 1])
            key = jnp.transpose(k_ref[:, cols])
            states.append(jnp.dot(
                jnp.concatenate([key, key], axis=1), jnp.concatenate([high, low], axis=0),
                preferred_element_type=jnp.float32,
            ))
            meta_ref[per_sub + i:per_sub + i + 1, :] = jnp.broadcast_to(carry[:, c:c + 1], (1, width))
        for i, state in enumerate(states):
            code, scale = to_code(state)
            code_ref[i] = code
            meta_ref[i:i + 1, :] = scale

    def send_pair(sub, turn, out, into, ss, rs, m_out, m_in, m_ss, m_rs, slot, peer):
        to = place(slab, peer)
        return [
            pltpu.make_async_remote_copy(
                src_ref=m_out.at[sub, slot], dst_ref=m_in.at[sub, me], send_sem=m_ss.at[sub, turn],
                recv_sem=m_rs.at[sub, me], device_id=to, device_id_type=MESH),
            pltpu.make_async_remote_copy(
                src_ref=out.at[sub, slot], dst_ref=into.at[sub, me], send_sem=ss.at[sub, turn],
                recv_sem=rs.at[sub, me], device_id=to, device_id_type=MESH),
        ]

    def state_pair(sub, turn):
        return send_pair(sub, turn, s_out, s_in, s_ss, s_rs, sm_out, sm_in, sm_ss, sm_rs, turn, other(me, turn))

    def prefix_pair(sub, turn):
        peer = other(me, turn)
        return send_pair(sub, turn, e_out, e_in, e_ss, e_rs, em_out, em_in, em_ss, em_rs, peer, peer)

    def wait_arrival(sub, number, into, rs, m_in, m_rs):
        for ref, sem in ((m_in, m_rs), (into, rs)):
            pltpu.make_async_remote_copy(
                src_ref=ref.at[sub, number], dst_ref=ref.at[sub, number], send_sem=sem.at[sub, number],
                recv_sem=sem.at[sub, number], device_id=place(slab, number), device_id_type=MESH,
            ).wait_recv()

    def send_states(sub):
        @pl.loop(0, GROUP - 1)
        def _(step):
            turn = turn_at(step)
            make_state(other(me, turn), sub, s_out.at[sub, turn], sm_out.at[sub, turn])
            for copy in state_pair(sub, turn):
                copy.start()

        make_state(me, sub, s_in.at[sub, me], sm_in.at[sub, me])

    def near_heads(low, high):
        @pl.loop(low, high)
        def _(g):
            sums = cum_t[g]
            for batch in range(0, per_owner, BATCH):
                few = range(batch, batch + BATCH)
                scores = [
                    lax.dot_general(
                        q_ref[:, columns(g, c)], k_ref[:, columns(g, c)], (((1,), (1,)), ((), ())),
                        preferred_element_type=jnp.float32,
                    )
                    for c in few
                ]
                weights = [
                    jnp.exp(
                        jnp.broadcast_to(sums[:, c:c + 1], (rows, rows))
                        - cum_rows[pl.ds(g * per_owner + c, 1), :] + bias[...]
                    )
                    for c in few
                ]
                parts = [halves(score * weight) for score, weight in zip(scores, weights)]
                results = []
                for c, (high_part, low_part) in zip(few, parts):
                    value = v_ref[:, columns(g, c)]
                    results.append(jnp.dot(
                        jnp.concatenate([high_part, low_part], axis=1),
                        jnp.concatenate([value, value], axis=0),
                        preferred_element_type=jnp.float32,
                    ))
                for c, result in zip(few, results):
                    near[:, columns(g, c)] = result

    def slab_totals(sub):
        @pl.loop(1, GROUP)
        def _(turn):
            wait_arrival(sub, other(me, turn), s_in, s_rs, sm_in, sm_rs)

        @pl.when(slab < slabs - 1)
        def _():
            @pl.loop(0, per_sub)
            def _(i):
                state = jnp.zeros((width, width), jnp.float32)
                for b in range(GROUP):
                    state = state * sm_in[sub, b, pl.ds(per_sub + i, 1), :] + from_code(s_in[sub, b, i]) * sm_in[
                        sub, b, pl.ds(i, 1), :]
                t_out[sub, i] = state

            total_copy(sub).start()

    def total_copy(sub):
        return pltpu.make_async_remote_copy(
            src_ref=t_out.at[sub], dst_ref=t_in.at[sub], send_sem=t_ss.at[sub], recv_sem=t_rs.at[sub],
            device_id=place(slab + 1, me), device_id_type=MESH)

    def send_prefixes(sub):
        @pl.when(slab > 0)
        def _():
            pltpu.make_async_remote_copy(
                src_ref=t_in.at[sub], dst_ref=t_in.at[sub], send_sem=t_ss.at[sub], recv_sem=t_rs.at[sub],
                device_id=place(slab - 1, me), device_id_type=MESH).wait_recv()

        @pl.when(slab == 0)
        def _():
            t_in[sub] = jnp.zeros(t_in.shape[1:], jnp.float32)

        @pl.loop(0, per_sub)
        def _(i):
            state = t_in[sub, i]
            for b in range(GROUP):
                code, scale = to_code(state)
                e_out[sub, b, i] = code
                em_out[sub, b, pl.ds(i, 1), :] = scale
                if b < GROUP - 1:
                    state = state * sm_in[sub, b, pl.ds(per_sub + i, 1), :] + from_code(s_in[sub, b, i]) * sm_in[
                        sub, b, pl.ds(i, 1), :]

        @pl.loop(0, GROUP - 1)
        def _(step):
            for copy in prefix_pair(sub, turn_at(step)):
                copy.start()

    def finish(g, sub, codes, metas):
        sums = cum_t[g]
        lead = jnp.exp(sums) * in_prior
        fars = []
        for i in range(per_sub):
            high, low = halves(from_code(codes[i]))
            query = q_ref[:, columns(g, sub * per_sub + i)]
            fars.append(jnp.dot(
                jnp.concatenate([query, query], axis=1), jnp.concatenate([high, low], axis=0),
                preferred_element_type=jnp.float32,
            ))
        mixes, squares = [], []
        for i, far in enumerate(fars):
            c = sub * per_sub + i
            mixed = near[:, columns(g, c)] + far * lead[:, c:c + 1] * metas[i:i + 1, :]
            mixes.append(mixed)
            squares.append(jnp.mean(mixed * mixed, axis=1, keepdims=True))
        for i, (mixed, square) in enumerate(zip(mixes, squares)):
            c = sub * per_sub + i
            gains = gain_all[pl.ds(g * per_owner + c, 1), :]
            o_ref[:, columns(g, c)] = (mixed * lax.rsqrt(square + 1e-06) * gains).astype(jnp.bfloat16)

    cum_rows = ld_all
    ld_all[...] = cum

    loads[0].wait()
    loads[1].wait()
    for sub in range(SUBS):
        send_states(sub)
    loads[2].wait()
    slab_totals(0)
    near_heads(0, 1)
    send_prefixes(0)
    near_heads(1, 3)
    slab_totals(1)
    near_heads(3, 4)
    send_prefixes(1)
    near_heads(4, GROUP)
    for sub in range(SUBS):
        finish(me, sub, e_out.at[sub, me], em_out.at[sub, me])

        @pl.loop(0, GROUP - 1)
        def _(step, sub=sub):
            g = other(me, turn_at(step))
            wait_arrival(sub, g, e_in, e_rs, em_in, em_rs)
            finish(g, sub, e_in.at[sub, g], em_in.at[sub, g])

    for sub in range(SUBS):
        @pl.loop(1, GROUP)
        def _(turn, sub=sub):
            for copy in state_pair(sub, turn) + prefix_pair(sub, turn):
                copy.wait_send()

        @pl.when(slab < slabs - 1)
        def _(sub=sub):
            total_copy(sub).wait_send()


def by_slabs(slabs, queries, keys, values, log_decay, doc_lengths, gain):
    rows, columns = queries.shape
    part = log_decay.shape[0]
    count = 2 * part
    per_sub = count // GROUP // SUBS
    width = columns // count
    codes = pltpu.VMEM((SUBS, GROUP, per_sub, width, width), jnp.int16)
    metas = pltpu.VMEM((SUBS, GROUP, 2 * per_sub, width), jnp.float32)
    totals = pltpu.VMEM((SUBS, per_sub, width, width), jnp.float32)
    sems = pltpu.SemaphoreType.DMA
    vmem = pl.BlockSpec(memory_space=pltpu.VMEM)
    return pl.pallas_call(
        functools.partial(slab_kernel, slabs),
        out_shape=jax.ShapeDtypeStruct((rows, columns), jnp.bfloat16),
        in_specs=[pl.BlockSpec(memory_space=pltpu.SMEM)] + [pl.BlockSpec(memory_space=pltpu.HBM)] * 3 + [vmem] * 2,
        out_specs=vmem,
        scratch_shapes=[pltpu.VMEM((rows, columns), jnp.bfloat16)] * 3 + [
            pltpu.VMEM((count, rows), jnp.float32),
            pltpu.VMEM((count, width), jnp.float32),
            pltpu.VMEM((GROUP, rows, count // GROUP), jnp.float32),
            pltpu.VMEM((rows, rows), jnp.float32),
            pltpu.VMEM((rows, columns), jnp.float32),
            codes, codes, metas, metas, codes, codes, metas, metas, totals, totals,
        ] + [sems((SUBS, GROUP))] * 8 + [sems((SUBS,))] * 2 + [sems((2,))] * 2 + [sems((3,))],
        compiler_params=pltpu.CompilerParams(
            collective_id=0, has_side_effects=True, vmem_limit_bytes=40 * 1024 * 1024
        ),
        cost_estimate=pl.CostEstimate(
            flops=14 * count * rows * rows * width, bytes_accessed=8 * rows * columns,
            transcendentals=count * rows * rows,
        ),
    )(doc_lengths, queries, keys, values, log_decay, gain.reshape(part, width))


def solution(mesh):
    devices = mesh.shape["seq"] * mesh.shape["head"]

    def run(queries, keys, values, log_decay, doc_lengths, gain):
        rows = queries.shape[0] // devices
        heads = log_decay.shape[0]
        width = queries.shape[1] // heads
        fits = (
            mesh.shape["head"] == 2 and devices % GROUP == 0 and rows == width == 128
            and GROUP * rows * 4 >= queries.shape[0] and heads % (GROUP * SUBS) == 0 and heads <= rows
        )
        body = functools.partial(by_slabs, devices // GROUP) if fits else local
        return jax.shard_map(
            body,
            mesh=mesh,
            in_specs=(
                P(("seq", "head"), None),
                P(("seq", "head"), None),
                P(("seq", "head"), None),
                P("head", "seq"),
                P(),
                P("head"),
            ),
            out_specs=P(("seq", "head"), None),
            check_vma=False,
        )(queries, keys, values, log_decay, doc_lengths, gain)

    return run
```

```python
import functools

import jax
import jax.numpy as jnp
from jax import lax
from jax.experimental import pallas as pl
from jax.experimental.pallas import tpu as pltpu
from jax.sharding import PartitionSpec as P

HIGHEST = lax.Precision.HIGHEST


def prefix(part, axis, combine, identity):
    place = lax.axis_index(axis)
    gathered = jax.tree.map(lambda a: lax.all_gather(a, axis), part)
    state = jax.tree.map(lambda a, e: jnp.zeros_like(a) + jnp.asarray(e, a.dtype), part, identity)

    def one(turn, state):
        return combine(
            state, jax.tree.map(lambda a: lax.dynamic_index_in_dim(a, turn, 0, False), gathered)
        )

    return lax.fori_loop(0, place, one, state)


def link(earlier, later):
    factor_one, state_one = earlier
    factor_two, state_two = later
    return (factor_one * factor_two, factor_two[:, None, None] * state_one + state_two)


def make_identity(amount, head_width):
    return (
        jnp.ones((amount,), jnp.float32),
        jnp.zeros((amount, head_width, head_width), jnp.float32),
    )


def local(queries, keys, values, log_decay, doc_lengths, gain):
    query_rows, key_rows, value_rows = (
        lax.all_to_all(queries, "head", split_axis=1, concat_axis=0, tiled=True),
        lax.all_to_all(keys, "head", split_axis=1, concat_axis=0, tiled=True),
        lax.all_to_all(values, "head", split_axis=1, concat_axis=0, tiled=True),
    )
    head_count = log_decay.shape[0]
    row_count = key_rows.shape[0]
    head_width = key_rows.shape[1] // head_count
    doc_ends = jnp.cumsum(doc_lengths)
    first_row = lax.axis_index("seq") * row_count
    positions = first_row + jnp.arange(row_count, dtype=jnp.int32)
    doc_ids = jnp.sum((doc_ends[None, :] <= positions[:, None]).astype(jnp.int32), axis=1)
    prior_doc = jnp.sum((doc_ends <= first_row - 1).astype(jnp.int32))
    order_ids = jnp.arange(row_count, dtype=jnp.int32)
    allowed = (order_ids[:, None] >= order_ids[None, :]) & (doc_ids[:, None] == doc_ids[None, :])
    decay_sum = jnp.cumsum(log_decay, axis=1)
    tailing = (
        jnp.exp(decay_sum[:, -1:] - decay_sum)
        * (doc_ids == doc_ids[-1]).astype(jnp.float32)[None, :]
    )
    leading = jnp.exp(decay_sum) * (doc_ids == prior_doc).astype(jnp.float32)[None, :]
    carried = jnp.exp(decay_sum[:, -1]) * (doc_ids[-1] == prior_doc).astype(jnp.float32)
    head_ids = jnp.arange(head_count, dtype=jnp.int32)

    def pick(block, head_index):
        return lax.dynamic_slice_in_dim(block, head_index * head_width, head_width, 1)

    def own_state(head_index):
        weighted = pick(key_rows, head_index).astype(jnp.float32) * tailing[head_index][:, None]
        value_part = pick(value_rows, head_index).astype(jnp.float32)
        return jnp.einsum(
            "jd,je->de", weighted, value_part, precision=HIGHEST, preferred_element_type=jnp.float32
        )

    def within(head_index):
        scores = lax.dot_general(
            pick(query_rows, head_index),
            pick(key_rows, head_index),
            (((1,), (1,)), ((), ())),
            preferred_element_type=jnp.float32,
        )
        gaps = decay_sum[head_index][:, None] - decay_sum[head_index][None, :]
        weights = jnp.where(allowed, jnp.exp(jnp.where(allowed, gaps, 0.0)), 0.0)
        value_part = pick(value_rows, head_index).astype(jnp.float32)
        return jnp.dot(
            scores * weights, value_part, precision=HIGHEST, preferred_element_type=jnp.float32
        )

    def across(paired):
        head_index, state = paired
        scaled = pick(query_rows, head_index).astype(jnp.float32) * leading[head_index][:, None]
        return jnp.dot(scaled, state, precision=HIGHEST, preferred_element_type=jnp.float32)

    own = lax.map(own_state, head_ids)
    total_factor, incoming = prefix(
        (carried, own), "seq", link, make_identity(head_count, head_width)
    )
    far = lax.map(across, (head_ids, incoming))
    near = lax.map(within, head_ids)
    mixed = near + far
    mean_square = jnp.mean(mixed * mixed, axis=-1, keepdims=True)
    normed = mixed * lax.rsqrt(mean_square + 1e-06) * gain.reshape(head_count, 1, head_width)
    merged = (
        jnp.transpose(normed, (1, 0, 2))
        .reshape(row_count, head_count * head_width)
        .astype(jnp.bfloat16)
    )
    return lax.all_to_all(merged, "head", split_axis=0, concat_axis=1, tiled=True)


MESH = pl.DeviceIdType.MESH
GROUP = 8
SUBS = 4
BATCH = 4
TOP = 32766.0
FAR_BELOW = -1e30
ORDER = (7, 6, 1, 5, 4, 3, 2)


def other(number, turn):
    out = 0
    for bit in (1, 2, 4):
        a, b = (number // bit) % 2, (turn // bit) % 2
        out = out + bit * (a + b - 2 * a * b)
    return out


def turn_at(step):
    out = 0
    for i, turn in enumerate(ORDER):
        out = out + jnp.where(step == i, turn, 0)
    return out


def halves(x):
    high = x.astype(jnp.bfloat16)
    return high, (x - high.astype(jnp.float32)).astype(jnp.bfloat16)


def to_code(state):
    scale = jnp.maximum(jnp.max(jnp.abs(state), axis=0, keepdims=True), 1e-30) * (1.0 / TOP)
    code = jnp.round(state * (1.0 / scale)).astype(jnp.int32).astype(jnp.int16)
    return code, scale


def from_code(code):
    return code.astype(jnp.int32).astype(jnp.float32)


def slab_kernel(
    slabs,
    doc_ref, q_far, k_far, v_far, ld_ref, gain_ref, o_ref,
    q_ref, k_ref, v_ref,
    ld_all, gain_all, cum_t, bias, near,
    s_out, s_in, sm_out, sm_in, e_out, e_in, em_out, em_in, t_out, t_in,
    s_ss, s_rs, sm_ss, sm_rs, e_ss, e_rs, em_ss, em_rs, t_ss, t_rs, x_ss, x_rs, l_s,
):
    seq, half = lax.axis_index("seq"), lax.axis_index("head")
    block = seq * 2 + half
    slab, me = block // GROUP, block % GROUP
    rows, width = q_ref.shape[0], q_ref.shape[0]
    part = ld_ref.shape[0]
    count = 2 * part
    per_owner = count // GROUP
    per_sub = per_owner // SUBS

    def place(other_slab, number):
        b = other_slab * GROUP + number
        return (b // 2, b % 2)

    loads = [
        pltpu.make_async_copy(far_ref, near_ref, l_s.at[i])
        for i, (far_ref, near_ref) in enumerate(((k_far, k_ref), (v_far, v_ref), (q_far, q_ref)))
    ]
    for load in loads:
        load.start()

    barrier = pltpu.get_barrier_semaphore()
    for turn in range(1, GROUP):
        pl.semaphore_signal(barrier, inc=1, device_id=place(slab, other(me, turn)), device_id_type=MESH)

    @pl.when(slab > 0)
    def _():
        pl.semaphore_signal(barrier, inc=1, device_id=place(slab - 1, me), device_id_type=MESH)

    @pl.when(slab < slabs - 1)
    def _():
        pl.semaphore_signal(barrier, inc=1, device_id=place(slab + 1, me), device_id_type=MESH)

    neighbours = GROUP - 1 + jnp.where(slab > 0, 1, 0) + jnp.where(slab < slabs - 1, 1, 0)
    pl.semaphore_wait(barrier, neighbours)

    mine = pl.ds(pl.multiple_of(half * part, part), part)
    swaps = [
        pltpu.make_async_remote_copy(
            src_ref=ld_ref.at[:, pl.ds(pl.multiple_of((1 - half) * rows, rows), rows)],
            dst_ref=ld_all.at[mine], send_sem=x_ss.at[0], recv_sem=x_rs.at[0],
            device_id=(seq, 1 - half), device_id_type=MESH),
        pltpu.make_async_remote_copy(
            src_ref=gain_ref, dst_ref=gain_all.at[mine], send_sem=x_ss.at[1], recv_sem=x_rs.at[1],
            device_id=(seq, 1 - half), device_id_type=MESH),
    ]
    for swap in swaps:
        swap.start()
    ld_all[mine, :] = ld_ref[:, pl.ds(pl.multiple_of(half * rows, rows), rows)]
    gain_all[mine, :] = gain_ref[...]

    first = block * rows
    down = lax.broadcasted_iota(jnp.int32, (rows, rows), 0)
    along = lax.broadcasted_iota(jnp.int32, (rows, rows), 1)
    doc_down = jnp.zeros((rows, rows), jnp.int32)
    doc_along = jnp.zeros((rows, rows), jnp.int32)
    prior = jnp.int32(0)
    final = jnp.int32(0)
    end = jnp.int32(0)
    for n in range(doc_ref.shape[0]):
        end = end + doc_ref[n]
        doc_down = doc_down + (down + first >= end).astype(jnp.int32)
        doc_along = doc_along + (along + first >= end).astype(jnp.int32)
        prior = prior + (end <= first - 1).astype(jnp.int32)
        final = final + (end <= first + rows - 1).astype(jnp.int32)
    bias[...] = jnp.where((down >= along) & (doc_down == doc_along), 0.0, FAR_BELOW)
    doc_few = doc_down[:, :per_owner]
    in_last = (doc_few == final).astype(jnp.float32)
    in_prior = (doc_few == prior).astype(jnp.float32)
    passes = (jnp.full((1, per_owner), final, jnp.int32) == prior).astype(jnp.float32)

    for swap in swaps:
        swap.wait()
    cum = jnp.dot(
        ld_all[...], (down <= along).astype(jnp.float32),
        precision=HIGHEST, preferred_element_type=jnp.float32,
    )
    turned = jnp.transpose(jnp.concatenate([cum, jnp.zeros((rows - count, rows), jnp.float32)], axis=0))
    for g in range(GROUP):
        cum_t[g] = turned[:, g * per_owner:(g + 1) * per_owner]

    def columns(g, c):
        return pl.ds(pl.multiple_of((g * per_owner + c) * width, width), width)

    def make_state(g, sub, code_ref, meta_ref):
        sums = cum_t[g]
        last = sums[rows - 1:rows, :]
        tail = jnp.exp(last - sums) * in_last
        carry = jnp.exp(last) * passes
        states = []
        for i in range(per_sub):
            c = sub * per_sub + i
            cols = columns(g, c)
            high, low = halves(v_ref[:, cols].astype(jnp.float32) * tail[:, c:c + 1])
            key = jnp.transpose(k_ref[:, cols])
            states.append(jnp.dot(
                jnp.concatenate([key, key], axis=1), jnp.concatenate([high, low], axis=0),
                preferred_element_type=jnp.float32,
            ))
            meta_ref[per_sub + i:per_sub + i + 1, :] = jnp.broadcast_to(carry[:, c:c + 1], (1, width))
        for i, state in enumerate(states):
            code, scale = to_code(state)
            code_ref[i] = code
            meta_ref[i:i + 1, :] = scale

    def send_pair(sub, turn, out, into, ss, rs, m_out, m_in, m_ss, m_rs, slot, peer):
        to = place(slab, peer)
        return [
            pltpu.make_async_remote_copy(
                src_ref=m_out.at[sub, slot], dst_ref=m_in.at[sub, me], send_sem=m_ss.at[sub, turn],
                recv_sem=m_rs.at[sub, me], device_id=to, device_id_type=MESH),
            pltpu.make_async_remote_copy(
                src_ref=out.at[sub, slot], dst_ref=into.at[sub, me], send_sem=ss.at[sub, turn],
                recv_sem=rs.at[sub, me], device_id=to, device_id_type=MESH),
        ]

    def state_pair(sub, turn):
        return send_pair(sub, turn, s_out, s_in, s_ss, s_rs, sm_out, sm_in, sm_ss, sm_rs, turn, other(me, turn))

    def prefix_pair(sub, turn):
        peer = other(me, turn)
        return send_pair(sub, turn, e_out, e_in, e_ss, e_rs, em_out, em_in, em_ss, em_rs, peer, peer)

    def wait_arrival(sub, number, into, rs, m_in, m_rs):
        for ref, sem in ((m_in, m_rs), (into, rs)):
            pltpu.make_async_remote_copy(
                src_ref=ref.at[sub, number], dst_ref=ref.at[sub, number], send_sem=sem.at[sub, number],
                recv_sem=sem.at[sub, number], device_id=place(slab, number), device_id_type=MESH,
            ).wait_recv()

    def send_states(sub):
        @pl.loop(0, GROUP - 1)
        def _(step):
            turn = turn_at(step)
            make_state(other(me, turn), sub, s_out.at[sub, turn], sm_out.at[sub, turn])
            for copy in state_pair(sub, turn):
                copy.start()

        make_state(me, sub, s_in.at[sub, me], sm_in.at[sub, me])

    def near_heads(low, high):
        @pl.loop(low, high)
        def _(g):
            sums = cum_t[g]
            for batch in range(0, per_owner, BATCH):
                few = range(batch, batch + BATCH)
                scores = [
                    lax.dot_general(
                        q_ref[:, columns(g, c)], k_ref[:, columns(g, c)], (((1,), (1,)), ((), ())),
                        preferred_element_type=jnp.float32,
                    )
                    for c in few
                ]
                weights = [
                    jnp.exp(
                        jnp.broadcast_to(sums[:, c:c + 1], (rows, rows))
                        - cum_rows[pl.ds(g * per_owner + c, 1), :] + bias[...]
                    )
                    for c in few
                ]
                parts = [halves(score * weight) for score, weight in zip(scores, weights)]
                results = []
                for c, (high_part, low_part) in zip(few, parts):
                    value = v_ref[:, columns(g, c)]
                    results.append(jnp.dot(
                        jnp.concatenate([high_part, low_part], axis=1),
                        jnp.concatenate([value, value], axis=0),
                        preferred_element_type=jnp.float32,
                    ))
                for c, result in zip(few, results):
                    near[:, columns(g, c)] = result

    def slab_totals(sub):
        @pl.loop(1, GROUP)
        def _(turn):
            wait_arrival(sub, other(me, turn), s_in, s_rs, sm_in, sm_rs)

        @pl.when(slab < slabs - 1)
        def _():
            @pl.loop(0, per_sub)
            def _(i):
                state = jnp.zeros((width, width), jnp.float32)
                for b in range(GROUP):
                    state = state * sm_in[sub, b, pl.ds(per_sub + i, 1), :] + from_code(s_in[sub, b, i]) * sm_in[
                        sub, b, pl.ds(i, 1), :]
                t_out[sub, i] = state

            total_copy(sub).start()

    def total_copy(sub):
        return pltpu.make_async_remote_copy(
            src_ref=t_out.at[sub], dst_ref=t_in.at[sub], send_sem=t_ss.at[sub], recv_sem=t_rs.at[sub],
            device_id=place(slab + 1, me), device_id_type=MESH)

    def send_prefixes(sub):
        @pl.when(slab > 0)
        def _():
            pltpu.make_async_remote_copy(
                src_ref=t_in.at[sub], dst_ref=t_in.at[sub], send_sem=t_ss.at[sub], recv_sem=t_rs.at[sub],
                device_id=place(slab - 1, me), device_id_type=MESH).wait_recv()

        @pl.when(slab == 0)
        def _():
            t_in[sub] = jnp.zeros(t_in.shape[1:], jnp.float32)

        @pl.loop(0, per_sub)
        def _(i):
            state = t_in[sub, i]
            for b in range(GROUP):
                code, scale = to_code(state)
                e_out[sub, b, i] = code
                em_out[sub, b, pl.ds(i, 1), :] = scale
                if b < GROUP - 1:
                    state = state * sm_in[sub, b, pl.ds(per_sub + i, 1), :] + from_code(s_in[sub, b, i]) * sm_in[
                        sub, b, pl.ds(i, 1), :]

        @pl.loop(0, GROUP - 1)
        def _(step):
            for copy in prefix_pair(sub, turn_at(step)):
                copy.start()

    def finish(g, sub, codes, metas):
        sums = cum_t[g]
        lead = jnp.exp(sums) * in_prior
        fars = []
        for i in range(per_sub):
            high, low = halves(from_code(codes[i]))
            query = q_ref[:, columns(g, sub * per_sub + i)]
            fars.append(jnp.dot(
                jnp.concatenate([query, query], axis=1), jnp.concatenate([high, low], axis=0),
                preferred_element_type=jnp.float32,
            ))
        mixes, squares = [], []
        for i, far in enumerate(fars):
            c = sub * per_sub + i
            mixed = near[:, columns(g, c)] + far * lead[:, c:c + 1] * metas[i:i + 1, :]
            mixes.append(mixed)
            squares.append(jnp.mean(mixed * mixed, axis=1, keepdims=True))
        for i, (mixed, square) in enumerate(zip(mixes, squares)):
            c = sub * per_sub + i
            gains = gain_all[pl.ds(g * per_owner + c, 1), :]
            o_ref[:, columns(g, c)] = (mixed * lax.rsqrt(square + 1e-06) * gains).astype(jnp.bfloat16)

    cum_rows = ld_all
    ld_all[...] = cum

    loads[0].wait()
    loads[1].wait()
    for sub in range(SUBS - 1):
        send_states(sub)
    slab_totals(0)
    send_states(SUBS - 1)
    slab_totals(1)
    loads[2].wait()
    send_prefixes(0)
    slab_totals(2)
    send_prefixes(1)
    near_heads(0, 1)
    slab_totals(3)
    send_prefixes(2)
    near_heads(1, 2)
    send_prefixes(3)
    near_heads(2, GROUP)
    for sub in range(SUBS):
        finish(me, sub, e_out.at[sub, me], em_out.at[sub, me])

        @pl.loop(0, GROUP - 1)
        def _(step, sub=sub):
            g = other(me, turn_at(step))
            wait_arrival(sub, g, e_in, e_rs, em_in, em_rs)
            finish(g, sub, e_in.at[sub, g], em_in.at[sub, g])

    for sub in range(SUBS):
        @pl.loop(1, GROUP)
        def _(turn, sub=sub):
            for copy in state_pair(sub, turn) + prefix_pair(sub, turn):
                copy.wait_send()

        @pl.when(slab < slabs - 1)
        def _(sub=sub):
            total_copy(sub).wait_send()


def by_slabs(slabs, queries, keys, values, log_decay, doc_lengths, gain):
    rows, columns = queries.shape
    part = log_decay.shape[0]
    count = 2 * part
    per_sub = count // GROUP // SUBS
    width = columns // count
    codes = pltpu.VMEM((SUBS, GROUP, per_sub, width, width), jnp.int16)
    metas = pltpu.VMEM((SUBS, GROUP, 2 * per_sub, width), jnp.float32)
    totals = pltpu.VMEM((SUBS, per_sub, width, width), jnp.float32)
    sems = pltpu.SemaphoreType.DMA
    vmem = pl.BlockSpec(memory_space=pltpu.VMEM)
    return pl.pallas_call(
        functools.partial(slab_kernel, slabs),
        out_shape=jax.ShapeDtypeStruct((rows, columns), jnp.bfloat16),
        in_specs=[pl.BlockSpec(memory_space=pltpu.SMEM)] + [pl.BlockSpec(memory_space=pltpu.HBM)] * 3 + [vmem] * 2,
        out_specs=vmem,
        scratch_shapes=[pltpu.VMEM((rows, columns), jnp.bfloat16)] * 3 + [
            pltpu.VMEM((count, rows), jnp.float32),
            pltpu.VMEM((count, width), jnp.float32),
            pltpu.VMEM((GROUP, rows, count // GROUP), jnp.float32),
            pltpu.VMEM((rows, rows), jnp.float32),
            pltpu.VMEM((rows, columns), jnp.float32),
            codes, codes, metas, metas, codes, codes, metas, metas, totals, totals,
        ] + [sems((SUBS, GROUP))] * 8 + [sems((SUBS,))] * 2 + [sems((2,))] * 2 + [sems((3,))],
        compiler_params=pltpu.CompilerParams(
            collective_id=0, has_side_effects=True, vmem_limit_bytes=58 * 1024 * 1024
        ),
        cost_estimate=pl.CostEstimate(
            flops=14 * count * rows * rows * width, bytes_accessed=8 * rows * columns,
            transcendentals=count * rows * rows,
        ),
    )(doc_lengths, queries, keys, values, log_decay, gain.reshape(part, width))


def solution(mesh):
    devices = mesh.shape["seq"] * mesh.shape["head"]

    def run(queries, keys, values, log_decay, doc_lengths, gain):
        rows = queries.shape[0] // devices
        heads = log_decay.shape[0]
        width = queries.shape[1] // heads
        fits = (
            mesh.shape["head"] == 2 and devices % GROUP == 0 and rows == width == 128
            and GROUP * rows * 4 >= queries.shape[0] and heads % (GROUP * SUBS) == 0 and heads <= rows
        )
        body = functools.partial(by_slabs, devices // GROUP) if fits else local
        return jax.shard_map(
            body,
            mesh=mesh,
            in_specs=(
                P(("seq", "head"), None),
                P(("seq", "head"), None),
                P(("seq", "head"), None),
                P("head", "seq"),
                P(),
                P("head"),
            ),
            out_specs=P(("seq", "head"), None),
            check_vma=False,
        )(queries, keys, values, log_decay, doc_lengths, gain)

    return run
```

```python
import functools

import jax
import jax.numpy as jnp
from jax import lax
from jax.experimental import pallas as pl
from jax.experimental.pallas import tpu as pltpu
from jax.sharding import PartitionSpec as P

HIGHEST = lax.Precision.HIGHEST


def prefix(part, axis, combine, identity):
    place = lax.axis_index(axis)
    gathered = jax.tree.map(lambda a: lax.all_gather(a, axis), part)
    state = jax.tree.map(lambda a, e: jnp.zeros_like(a) + jnp.asarray(e, a.dtype), part, identity)

    def one(turn, state):
        return combine(
            state, jax.tree.map(lambda a: lax.dynamic_index_in_dim(a, turn, 0, False), gathered)
        )

    return lax.fori_loop(0, place, one, state)


def link(earlier, later):
    factor_one, state_one = earlier
    factor_two, state_two = later
    return (factor_one * factor_two, factor_two[:, None, None] * state_one + state_two)


def make_identity(amount, head_width):
    return (
        jnp.ones((amount,), jnp.float32),
        jnp.zeros((amount, head_width, head_width), jnp.float32),
    )


def local(queries, keys, values, log_decay, doc_lengths, gain):
    query_rows, key_rows, value_rows = (
        lax.all_to_all(queries, "head", split_axis=1, concat_axis=0, tiled=True),
        lax.all_to_all(keys, "head", split_axis=1, concat_axis=0, tiled=True),
        lax.all_to_all(values, "head", split_axis=1, concat_axis=0, tiled=True),
    )
    head_count = log_decay.shape[0]
    row_count = key_rows.shape[0]
    head_width = key_rows.shape[1] // head_count
    doc_ends = jnp.cumsum(doc_lengths)
    first_row = lax.axis_index("seq") * row_count
    positions = first_row + jnp.arange(row_count, dtype=jnp.int32)
    doc_ids = jnp.sum((doc_ends[None, :] <= positions[:, None]).astype(jnp.int32), axis=1)
    prior_doc = jnp.sum((doc_ends <= first_row - 1).astype(jnp.int32))
    order_ids = jnp.arange(row_count, dtype=jnp.int32)
    allowed = (order_ids[:, None] >= order_ids[None, :]) & (doc_ids[:, None] == doc_ids[None, :])
    decay_sum = jnp.cumsum(log_decay, axis=1)
    tailing = (
        jnp.exp(decay_sum[:, -1:] - decay_sum)
        * (doc_ids == doc_ids[-1]).astype(jnp.float32)[None, :]
    )
    leading = jnp.exp(decay_sum) * (doc_ids == prior_doc).astype(jnp.float32)[None, :]
    carried = jnp.exp(decay_sum[:, -1]) * (doc_ids[-1] == prior_doc).astype(jnp.float32)
    head_ids = jnp.arange(head_count, dtype=jnp.int32)

    def pick(block, head_index):
        return lax.dynamic_slice_in_dim(block, head_index * head_width, head_width, 1)

    def own_state(head_index):
        weighted = pick(key_rows, head_index).astype(jnp.float32) * tailing[head_index][:, None]
        value_part = pick(value_rows, head_index).astype(jnp.float32)
        return jnp.einsum(
            "jd,je->de", weighted, value_part, precision=HIGHEST, preferred_element_type=jnp.float32
        )

    def within(head_index):
        scores = lax.dot_general(
            pick(query_rows, head_index),
            pick(key_rows, head_index),
            (((1,), (1,)), ((), ())),
            preferred_element_type=jnp.float32,
        )
        gaps = decay_sum[head_index][:, None] - decay_sum[head_index][None, :]
        weights = jnp.where(allowed, jnp.exp(jnp.where(allowed, gaps, 0.0)), 0.0)
        value_part = pick(value_rows, head_index).astype(jnp.float32)
        return jnp.dot(
            scores * weights, value_part, precision=HIGHEST, preferred_element_type=jnp.float32
        )

    def across(paired):
        head_index, state = paired
        scaled = pick(query_rows, head_index).astype(jnp.float32) * leading[head_index][:, None]
        return jnp.dot(scaled, state, precision=HIGHEST, preferred_element_type=jnp.float32)

    own = lax.map(own_state, head_ids)
    total_factor, incoming = prefix(
        (carried, own), "seq", link, make_identity(head_count, head_width)
    )
    far = lax.map(across, (head_ids, incoming))
    near = lax.map(within, head_ids)
    mixed = near + far
    mean_square = jnp.mean(mixed * mixed, axis=-1, keepdims=True)
    normed = mixed * lax.rsqrt(mean_square + 1e-06) * gain.reshape(head_count, 1, head_width)
    merged = (
        jnp.transpose(normed, (1, 0, 2))
        .reshape(row_count, head_count * head_width)
        .astype(jnp.bfloat16)
    )
    return lax.all_to_all(merged, "head", split_axis=0, concat_axis=1, tiled=True)


MESH = pl.DeviceIdType.MESH
GROUP = 8
SUBS = 2
BATCH = 4
TOP = 32766.0
NEAREST = 12582912.0
FAR_BELOW = -1e30
ORDER = (7, 6, 1, 5, 4, 3, 2)


def other(number, turn):
    out = 0
    for bit in (1, 2, 4):
        a, b = (number // bit) % 2, (turn // bit) % 2
        out = out + bit * (a + b - 2 * a * b)
    return out


def turn_at(step):
    out = 0
    for i, turn in enumerate(ORDER):
        out = out + jnp.where(step == i, turn, 0)
    return out


def halves(x):
    high = x.astype(jnp.bfloat16)
    return high, (x - high.astype(jnp.float32)).astype(jnp.bfloat16)


def to_code(state):
    scale = jnp.maximum(jnp.max(jnp.abs(state), axis=0, keepdims=True), 1e-30) * (1.0 / TOP)
    code = (state * (1.0 / scale) + NEAREST - NEAREST).astype(jnp.int32).astype(jnp.int16)
    return code, scale


def from_code(code):
    return code.astype(jnp.int32).astype(jnp.float32)


def slab_kernel(
    slabs,
    doc_ref, q_far, k_far, v_far, ld_ref, gain_ref, o_ref,
    q_ref, k_ref, v_ref, keys_turned,
    ld_all, gain_all, cum_t, bias, near,
    s_out, s_in, sm_out, sm_in, e_out, e_in, em_out, em_in, t_out, t_in,
    s_ss, s_rs, sm_ss, sm_rs, e_ss, e_rs, em_ss, em_rs, t_ss, t_rs, x_ss, x_rs, l_s,
):
    seq, half = lax.axis_index("seq"), lax.axis_index("head")
    block = seq * 2 + half
    slab, me = block // GROUP, block % GROUP
    rows, width = q_ref.shape[0], q_ref.shape[0]
    part = ld_ref.shape[0]
    count = 2 * part
    per_owner = count // GROUP
    per_sub = per_owner // SUBS

    def place(other_slab, number):
        b = other_slab * GROUP + number
        return (b // 2, b % 2)

    loads = [
        pltpu.make_async_copy(far_ref, near_ref, l_s.at[i])
        for i, (far_ref, near_ref) in enumerate(((k_far, k_ref), (v_far, v_ref), (q_far, q_ref)))
    ]
    for load in loads:
        load.start()

    barrier = pltpu.get_barrier_semaphore()
    for turn in range(1, GROUP):
        pl.semaphore_signal(barrier, inc=1, device_id=place(slab, other(me, turn)), device_id_type=MESH)

    @pl.when(slab > 0)
    def _():
        pl.semaphore_signal(barrier, inc=1, device_id=place(slab - 1, me), device_id_type=MESH)

    @pl.when(slab < slabs - 1)
    def _():
        pl.semaphore_signal(barrier, inc=1, device_id=place(slab + 1, me), device_id_type=MESH)

    neighbours = GROUP - 1 + jnp.where(slab > 0, 1, 0) + jnp.where(slab < slabs - 1, 1, 0)
    pl.semaphore_wait(barrier, neighbours)

    mine = pl.ds(pl.multiple_of(half * part, part), part)
    swaps = [
        pltpu.make_async_remote_copy(
            src_ref=ld_ref.at[:, pl.ds(pl.multiple_of((1 - half) * rows, rows), rows)],
            dst_ref=ld_all.at[mine], send_sem=x_ss.at[0], recv_sem=x_rs.at[0],
            device_id=(seq, 1 - half), device_id_type=MESH),
        pltpu.make_async_remote_copy(
            src_ref=gain_ref, dst_ref=gain_all.at[mine], send_sem=x_ss.at[1], recv_sem=x_rs.at[1],
            device_id=(seq, 1 - half), device_id_type=MESH),
    ]
    for swap in swaps:
        swap.start()
    ld_all[mine, :] = ld_ref[:, pl.ds(pl.multiple_of(half * rows, rows), rows)]
    gain_all[mine, :] = gain_ref[...]

    first = block * rows
    down = lax.broadcasted_iota(jnp.int32, (rows, rows), 0)
    along = lax.broadcasted_iota(jnp.int32, (rows, rows), 1)
    doc_down = jnp.zeros((rows, rows), jnp.int32)
    doc_along = jnp.zeros((rows, rows), jnp.int32)
    prior = jnp.int32(0)
    final = jnp.int32(0)
    end = jnp.int32(0)
    for n in range(doc_ref.shape[0]):
        end = end + doc_ref[n]
        doc_down = doc_down + (down + first >= end).astype(jnp.int32)
        doc_along = doc_along + (along + first >= end).astype(jnp.int32)
        prior = prior + (end <= first - 1).astype(jnp.int32)
        final = final + (end <= first + rows - 1).astype(jnp.int32)
    bias[...] = jnp.where((down >= along) & (doc_down == doc_along), 0.0, FAR_BELOW)
    doc_few = doc_down[:, :per_owner]
    in_last = (doc_few == final).astype(jnp.float32)
    in_prior = (doc_few == prior).astype(jnp.float32)
    passes = (jnp.full((1, per_owner), final, jnp.int32) == prior).astype(jnp.float32)

    for swap in swaps:
        swap.wait()
    cum = jnp.dot(
        ld_all[...], (down <= along).astype(jnp.float32),
        precision=HIGHEST, preferred_element_type=jnp.float32,
    )
    turned = jnp.transpose(jnp.concatenate([cum, jnp.zeros((rows - count, rows), jnp.float32)], axis=0))
    for g in range(GROUP):
        cum_t[g] = turned[:, g * per_owner:(g + 1) * per_owner]

    def columns(g, c):
        return pl.ds(pl.multiple_of((g * per_owner + c) * width, width), width)

    def make_state(g, sub, code_ref, meta_ref):
        sums = cum_t[g]
        last = sums[rows - 1:rows, :]
        tail = jnp.exp(last - sums) * in_last
        carry = jnp.exp(last) * passes
        states = []
        for i in range(per_sub):
            c = sub * per_sub + i
            cols = columns(g, c)
            high, low = halves(v_ref[:, cols].astype(jnp.float32) * tail[:, c:c + 1])
            key = jnp.transpose(k_ref[:, cols])
            keys_turned[g * per_owner + c] = key
            states.append(jnp.dot(
                jnp.concatenate([key, key], axis=1), jnp.concatenate([high, low], axis=0),
                preferred_element_type=jnp.float32,
            ))
            meta_ref[per_sub + i:per_sub + i + 1, :] = jnp.broadcast_to(carry[:, c:c + 1], (1, width))
        for i, state in enumerate(states):
            code, scale = to_code(state)
            code_ref[i] = code
            meta_ref[i:i + 1, :] = scale

    def send_pair(sub, turn, out, into, ss, rs, m_out, m_in, m_ss, m_rs, slot, peer):
        to = place(slab, peer)
        return [
            pltpu.make_async_remote_copy(
                src_ref=m_out.at[sub, slot], dst_ref=m_in.at[sub, me], send_sem=m_ss.at[sub, turn],
                recv_sem=m_rs.at[sub, me], device_id=to, device_id_type=MESH),
            pltpu.make_async_remote_copy(
                src_ref=out.at[sub, slot], dst_ref=into.at[sub, me], send_sem=ss.at[sub, turn],
                recv_sem=rs.at[sub, me], device_id=to, device_id_type=MESH),
        ]

    def state_pair(sub, turn):
        return send_pair(sub, turn, s_out, s_in, s_ss, s_rs, sm_out, sm_in, sm_ss, sm_rs, turn, other(me, turn))

    def prefix_pair(sub, turn):
        peer = other(me, turn)
        return send_pair(sub, turn, e_out, e_in, e_ss, e_rs, em_out, em_in, em_ss, em_rs, peer, peer)

    def wait_arrival(sub, number, into, rs, m_in, m_rs):
        for ref, sem in ((m_in, m_rs), (into, rs)):
            pltpu.make_async_remote_copy(
                src_ref=ref.at[sub, number], dst_ref=ref.at[sub, number], send_sem=sem.at[sub, number],
                recv_sem=sem.at[sub, number], device_id=place(slab, number), device_id_type=MESH,
            ).wait_recv()

    def send_states(sub):
        @pl.loop(0, GROUP - 1)
        def _(step):
            turn = turn_at(step)
            make_state(other(me, turn), sub, s_out.at[sub, turn], sm_out.at[sub, turn])
            for copy in state_pair(sub, turn):
                copy.start()

        make_state(me, sub, s_in.at[sub, me], sm_in.at[sub, me])

    def near_heads(low, high):
        @pl.loop(low, high)
        def _(g):
            sums = cum_t[g]
            for batch in range(0, per_owner, BATCH):
                few = range(batch, batch + BATCH)
                scores = [
                    jnp.dot(
                        q_ref[:, columns(g, c)], keys_turned[g * per_owner + c],
                        preferred_element_type=jnp.float32,
                    )
                    for c in few
                ]
                weights = [
                    jnp.exp(
                        jnp.broadcast_to(sums[:, c:c + 1], (rows, rows))
                        - cum_rows[pl.ds(g * per_owner + c, 1), :] + bias[...]
                    )
                    for c in few
                ]
                parts = [halves(score * weight) for score, weight in zip(scores, weights)]
                results = []
                for c, (high_part, low_part) in zip(few, parts):
                    value = v_ref[:, columns(g, c)]
                    results.append(jnp.dot(
                        jnp.concatenate([high_part, low_part], axis=1),
                        jnp.concatenate([value, value], axis=0),
                        preferred_element_type=jnp.float32,
                    ))
                for c, result in zip(few, results):
                    near[:, columns(g, c)] = result

    def slab_totals(sub):
        @pl.loop(1, GROUP)
        def _(turn):
            wait_arrival(sub, other(me, turn), s_in, s_rs, sm_in, sm_rs)

        @pl.when(slab < slabs - 1)
        def _():
            @pl.loop(0, per_sub)
            def _(i):
                state = jnp.zeros((width, width), jnp.float32)
                for b in range(GROUP):
                    state = state * sm_in[sub, b, pl.ds(per_sub + i, 1), :] + from_code(s_in[sub, b, i]) * sm_in[
                        sub, b, pl.ds(i, 1), :]
                t_out[sub, i] = state

            total_copy(sub).start()

    def total_copy(sub):
        return pltpu.make_async_remote_copy(
            src_ref=t_out.at[sub], dst_ref=t_in.at[sub], send_sem=t_ss.at[sub], recv_sem=t_rs.at[sub],
            device_id=place(slab + 1, me), device_id_type=MESH)

    def send_prefixes(sub):
        @pl.when(slab > 0)
        def _():
            pltpu.make_async_remote_copy(
                src_ref=t_in.at[sub], dst_ref=t_in.at[sub], send_sem=t_ss.at[sub], recv_sem=t_rs.at[sub],
                device_id=place(slab - 1, me), device_id_type=MESH).wait_recv()

        @pl.when(slab == 0)
        def _():
            t_in[sub] = jnp.zeros(t_in.shape[1:], jnp.float32)

        @pl.loop(0, per_sub)
        def _(i):
            state = t_in[sub, i]
            for b in range(GROUP):
                code, scale = to_code(state)
                e_out[sub, b, i] = code
                em_out[sub, b, pl.ds(i, 1), :] = scale
                if b < GROUP - 1:
                    state = state * sm_in[sub, b, pl.ds(per_sub + i, 1), :] + from_code(s_in[sub, b, i]) * sm_in[
                        sub, b, pl.ds(i, 1), :]

        @pl.loop(0, GROUP - 1)
        def _(step):
            for copy in prefix_pair(sub, turn_at(step)):
                copy.start()

    def finish(g, sub, codes, metas):
        sums = cum_t[g]
        lead = jnp.exp(sums) * in_prior
        fars = []
        for i in range(per_sub):
            high, low = halves(from_code(codes[i]))
            query = q_ref[:, columns(g, sub * per_sub + i)]
            fars.append(jnp.dot(
                jnp.concatenate([query, query], axis=1), jnp.concatenate([high, low], axis=0),
                preferred_element_type=jnp.float32,
            ))
        mixes, squares = [], []
        for i, far in enumerate(fars):
            c = sub * per_sub + i
            mixed = near[:, columns(g, c)] + far * lead[:, c:c + 1] * metas[i:i + 1, :]
            mixes.append(mixed)
            squares.append(jnp.mean(mixed * mixed, axis=1, keepdims=True))
        for i, (mixed, square) in enumerate(zip(mixes, squares)):
            c = sub * per_sub + i
            gains = gain_all[pl.ds(g * per_owner + c, 1), :]
            o_ref[:, columns(g, c)] = (mixed * lax.rsqrt(square + 1e-06) * gains).astype(jnp.bfloat16)

    cum_rows = ld_all
    ld_all[...] = cum

    loads[0].wait()
    loads[1].wait()
    for sub in range(SUBS):
        send_states(sub)
    loads[2].wait()
    slab_totals(0)
    near_heads(0, 2)
    send_prefixes(0)
    near_heads(2, 3)
    slab_totals(1)
    near_heads(3, 5)
    send_prefixes(1)
    near_heads(5, GROUP)
    for sub in range(SUBS):
        finish(me, sub, e_out.at[sub, me], em_out.at[sub, me])

        @pl.loop(0, GROUP - 1)
        def _(step, sub=sub):
            g = other(me, turn_at(step))
            wait_arrival(sub, g, e_in, e_rs, em_in, em_rs)
            finish(g, sub, e_in.at[sub, g], em_in.at[sub, g])

    for sub in range(SUBS):
        @pl.loop(1, GROUP)
        def _(turn, sub=sub):
            for copy in state_pair(sub, turn) + prefix_pair(sub, turn):
                copy.wait_send()

        @pl.when(slab < slabs - 1)
        def _(sub=sub):
            total_copy(sub).wait_send()


def by_slabs(slabs, queries, keys, values, log_decay, doc_lengths, gain):
    rows, columns = queries.shape
    part = log_decay.shape[0]
    count = 2 * part
    per_sub = count // GROUP // SUBS
    width = columns // count
    codes = pltpu.VMEM((SUBS, GROUP, per_sub, width, width), jnp.int16)
    metas = pltpu.VMEM((SUBS, GROUP, 2 * per_sub, width), jnp.float32)
    totals = pltpu.VMEM((SUBS, per_sub, width, width), jnp.float32)
    sems = pltpu.SemaphoreType.DMA
    vmem = pl.BlockSpec(memory_space=pltpu.VMEM)
    return pl.pallas_call(
        functools.partial(slab_kernel, slabs),
        out_shape=jax.ShapeDtypeStruct((rows, columns), jnp.bfloat16),
        in_specs=[pl.BlockSpec(memory_space=pltpu.SMEM)] + [pl.BlockSpec(memory_space=pltpu.HBM)] * 3 + [vmem] * 2,
        out_specs=vmem,
        scratch_shapes=[pltpu.VMEM((rows, columns), jnp.bfloat16)] * 3 + [
            pltpu.VMEM((count, width, rows), jnp.bfloat16),
            pltpu.VMEM((count, rows), jnp.float32),
            pltpu.VMEM((count, width), jnp.float32),
            pltpu.VMEM((GROUP, rows, count // GROUP), jnp.float32),
            pltpu.VMEM((rows, rows), jnp.float32),
            pltpu.VMEM((rows, columns), jnp.float32),
            codes, codes, metas, metas, codes, codes, metas, metas, totals, totals,
        ] + [sems((SUBS, GROUP))] * 8 + [sems((SUBS,))] * 2 + [sems((2,))] * 2 + [sems((3,))],
        compiler_params=pltpu.CompilerParams(
            collective_id=0, has_side_effects=True, vmem_limit_bytes=58 * 1024 * 1024
        ),
        cost_estimate=pl.CostEstimate(
            flops=14 * count * rows * rows * width, bytes_accessed=8 * rows * columns,
            transcendentals=count * rows * rows,
        ),
    )(doc_lengths, queries, keys, values, log_decay, gain.reshape(part, width))


def solution(mesh):
    devices = mesh.shape["seq"] * mesh.shape["head"]

    def run(queries, keys, values, log_decay, doc_lengths, gain):
        rows = queries.shape[0] // devices
        heads = log_decay.shape[0]
        width = queries.shape[1] // heads
        fits = (
            mesh.shape["head"] == 2 and devices % GROUP == 0 and rows == width == 128
            and GROUP * rows * 4 >= queries.shape[0] and heads % (GROUP * SUBS) == 0 and heads <= rows
        )
        body = functools.partial(by_slabs, devices // GROUP) if fits else local
        return jax.shard_map(
            body,
            mesh=mesh,
            in_specs=(
                P(("seq", "head"), None),
                P(("seq", "head"), None),
                P(("seq", "head"), None),
                P("head", "seq"),
                P(),
                P("head"),
            ),
            out_specs=P(("seq", "head"), None),
            check_vma=False,
        )(queries, keys, values, log_decay, doc_lengths, gain)

    return run
```

```python
import functools

import jax
import jax.numpy as jnp
from jax import lax
from jax.experimental import pallas as pl
from jax.experimental.pallas import tpu as pltpu
from jax.sharding import PartitionSpec as P

HIGHEST = lax.Precision.HIGHEST


def prefix(part, axis, combine, identity):
    place = lax.axis_index(axis)
    gathered = jax.tree.map(lambda a: lax.all_gather(a, axis), part)
    state = jax.tree.map(lambda a, e: jnp.zeros_like(a) + jnp.asarray(e, a.dtype), part, identity)

    def one(turn, state):
        return combine(
            state, jax.tree.map(lambda a: lax.dynamic_index_in_dim(a, turn, 0, False), gathered)
        )

    return lax.fori_loop(0, place, one, state)


def link(earlier, later):
    factor_one, state_one = earlier
    factor_two, state_two = later
    return (factor_one * factor_two, factor_two[:, None, None] * state_one + state_two)


def make_identity(amount, head_width):
    return (
        jnp.ones((amount,), jnp.float32),
        jnp.zeros((amount, head_width, head_width), jnp.float32),
    )


def local(queries, keys, values, log_decay, doc_lengths, gain):
    query_rows, key_rows, value_rows = (
        lax.all_to_all(queries, "head", split_axis=1, concat_axis=0, tiled=True),
        lax.all_to_all(keys, "head", split_axis=1, concat_axis=0, tiled=True),
        lax.all_to_all(values, "head", split_axis=1, concat_axis=0, tiled=True),
    )
    head_count = log_decay.shape[0]
    row_count = key_rows.shape[0]
    head_width = key_rows.shape[1] // head_count
    doc_ends = jnp.cumsum(doc_lengths)
    first_row = lax.axis_index("seq") * row_count
    positions = first_row + jnp.arange(row_count, dtype=jnp.int32)
    doc_ids = jnp.sum((doc_ends[None, :] <= positions[:, None]).astype(jnp.int32), axis=1)
    prior_doc = jnp.sum((doc_ends <= first_row - 1).astype(jnp.int32))
    order_ids = jnp.arange(row_count, dtype=jnp.int32)
    allowed = (order_ids[:, None] >= order_ids[None, :]) & (doc_ids[:, None] == doc_ids[None, :])
    decay_sum = jnp.cumsum(log_decay, axis=1)
    tailing = (
        jnp.exp(decay_sum[:, -1:] - decay_sum)
        * (doc_ids == doc_ids[-1]).astype(jnp.float32)[None, :]
    )
    leading = jnp.exp(decay_sum) * (doc_ids == prior_doc).astype(jnp.float32)[None, :]
    carried = jnp.exp(decay_sum[:, -1]) * (doc_ids[-1] == prior_doc).astype(jnp.float32)
    head_ids = jnp.arange(head_count, dtype=jnp.int32)

    def pick(block, head_index):
        return lax.dynamic_slice_in_dim(block, head_index * head_width, head_width, 1)

    def own_state(head_index):
        weighted = pick(key_rows, head_index).astype(jnp.float32) * tailing[head_index][:, None]
        value_part = pick(value_rows, head_index).astype(jnp.float32)
        return jnp.einsum(
            "jd,je->de", weighted, value_part, precision=HIGHEST, preferred_element_type=jnp.float32
        )

    def within(head_index):
        scores = lax.dot_general(
            pick(query_rows, head_index),
            pick(key_rows, head_index),
            (((1,), (1,)), ((), ())),
            preferred_element_type=jnp.float32,
        )
        gaps = decay_sum[head_index][:, None] - decay_sum[head_index][None, :]
        weights = jnp.where(allowed, jnp.exp(jnp.where(allowed, gaps, 0.0)), 0.0)
        value_part = pick(value_rows, head_index).astype(jnp.float32)
        return jnp.dot(
            scores * weights, value_part, precision=HIGHEST, preferred_element_type=jnp.float32
        )

    def across(paired):
        head_index, state = paired
        scaled = pick(query_rows, head_index).astype(jnp.float32) * leading[head_index][:, None]
        return jnp.dot(scaled, state, precision=HIGHEST, preferred_element_type=jnp.float32)

    own = lax.map(own_state, head_ids)
    total_factor, incoming = prefix(
        (carried, own), "seq", link, make_identity(head_count, head_width)
    )
    far = lax.map(across, (head_ids, incoming))
    near = lax.map(within, head_ids)
    mixed = near + far
    mean_square = jnp.mean(mixed * mixed, axis=-1, keepdims=True)
    normed = mixed * lax.rsqrt(mean_square + 1e-06) * gain.reshape(head_count, 1, head_width)
    merged = (
        jnp.transpose(normed, (1, 0, 2))
        .reshape(row_count, head_count * head_width)
        .astype(jnp.bfloat16)
    )
    return lax.all_to_all(merged, "head", split_axis=0, concat_axis=1, tiled=True)


MESH = pl.DeviceIdType.MESH
GROUP = 8
SUBS = 2
BATCH = 4
TOP = 32766.0
NEAREST = 12582912.0
FAR_BELOW = -1e30
ORDER = (7, 6, 1, 5, 4, 3, 2)


def other(number, turn):
    out = 0
    for bit in (1, 2, 4):
        a, b = (number // bit) % 2, (turn // bit) % 2
        out = out + bit * (a + b - 2 * a * b)
    return out


def turn_at(step):
    out = 0
    for i, turn in enumerate(ORDER):
        out = out + jnp.where(step == i, turn, 0)
    return out


def halves(x):
    high = x.astype(jnp.bfloat16)
    return high, (x - high.astype(jnp.float32)).astype(jnp.bfloat16)


def to_code(state):
    scale = jnp.maximum(jnp.max(jnp.abs(state), axis=0, keepdims=True), 1e-30) * (1.0 / TOP)
    code = (state * (1.0 / scale) + NEAREST - NEAREST).astype(jnp.int32).astype(jnp.int16)
    return code, scale


def from_code(code):
    return code.astype(jnp.int32).astype(jnp.float32)


def slab_kernel(
    slabs,
    doc_ref, q_far, k_far, v_far, ld_ref, gain_ref, o_ref,
    q_ref, k_ref, v_ref, keys_turned,
    ld_all, gain_all, cum_t, bias, near,
    s_out, s_in, sm_out, sm_in, e_out, e_in, em_out, em_in, t_out, t_in,
    s_ss, s_rs, sm_ss, sm_rs, e_ss, e_rs, em_ss, em_rs, t_ss, t_rs, x_ss, x_rs, l_s,
):
    seq, half = lax.axis_index("seq"), lax.axis_index("head")
    block = seq * 2 + half
    slab, me = block // GROUP, block % GROUP
    rows, width = q_ref.shape[0], q_ref.shape[0]
    part = ld_ref.shape[0]
    count = 2 * part
    per_owner = count // GROUP
    per_sub = per_owner // SUBS

    def place(other_slab, number):
        b = other_slab * GROUP + number
        return (b // 2, b % 2)

    loads = [
        pltpu.make_async_copy(far_ref, near_ref, l_s.at[i])
        for i, (far_ref, near_ref) in enumerate(((k_far, k_ref), (v_far, v_ref), (q_far, q_ref)))
    ]
    for load in loads:
        load.start()

    barrier = pltpu.get_barrier_semaphore()
    for turn in range(1, GROUP):
        pl.semaphore_signal(barrier, inc=1, device_id=place(slab, other(me, turn)), device_id_type=MESH)

    @pl.when(slab > 0)
    def _():
        pl.semaphore_signal(barrier, inc=1, device_id=place(slab - 1, me), device_id_type=MESH)

    @pl.when(slab < slabs - 1)
    def _():
        pl.semaphore_signal(barrier, inc=1, device_id=place(slab + 1, me), device_id_type=MESH)

    neighbours = GROUP - 1 + jnp.where(slab > 0, 1, 0) + jnp.where(slab < slabs - 1, 1, 0)
    pl.semaphore_wait(barrier, neighbours)

    mine = pl.ds(pl.multiple_of(half * part, part), part)
    swaps = [
        pltpu.make_async_remote_copy(
            src_ref=ld_ref.at[:, pl.ds(pl.multiple_of((1 - half) * rows, rows), rows)],
            dst_ref=ld_all.at[mine], send_sem=x_ss.at[0], recv_sem=x_rs.at[0],
            device_id=(seq, 1 - half), device_id_type=MESH),
        pltpu.make_async_remote_copy(
            src_ref=gain_ref, dst_ref=gain_all.at[mine], send_sem=x_ss.at[1], recv_sem=x_rs.at[1],
            device_id=(seq, 1 - half), device_id_type=MESH),
    ]
    for swap in swaps:
        swap.start()
    ld_all[mine, :] = ld_ref[:, pl.ds(pl.multiple_of(half * rows, rows), rows)]
    gain_all[mine, :] = gain_ref[...]

    first = block * rows
    down = lax.broadcasted_iota(jnp.int32, (rows, rows), 0)
    along = lax.broadcasted_iota(jnp.int32, (rows, rows), 1)
    doc_down = jnp.zeros((rows, rows), jnp.int32)
    doc_along = jnp.zeros((rows, rows), jnp.int32)
    prior = jnp.int32(0)
    final = jnp.int32(0)
    end = jnp.int32(0)
    for n in range(doc_ref.shape[0]):
        end = end + doc_ref[n]
        doc_down = doc_down + (down + first >= end).astype(jnp.int32)
        doc_along = doc_along + (along + first >= end).astype(jnp.int32)
        prior = prior + (end <= first - 1).astype(jnp.int32)
        final = final + (end <= first + rows - 1).astype(jnp.int32)
    bias[...] = jnp.where((down >= along) & (doc_down == doc_along), 0.0, FAR_BELOW)
    doc_few = doc_down[:, :per_owner]
    in_last = (doc_few == final).astype(jnp.float32)
    in_prior = (doc_few == prior).astype(jnp.float32)
    passes = (jnp.full((1, per_owner), final, jnp.int32) == prior).astype(jnp.float32)

    for swap in swaps:
        swap.wait()
    cum = jnp.dot(
        ld_all[...], (down <= along).astype(jnp.float32),
        precision=HIGHEST, preferred_element_type=jnp.float32,
    )
    turned = jnp.transpose(jnp.concatenate([cum, jnp.zeros((rows - count, rows), jnp.float32)], axis=0))
    for g in range(GROUP):
        cum_t[g] = turned[:, g * per_owner:(g + 1) * per_owner]

    def columns(g, c):
        return pl.ds(pl.multiple_of((g * per_owner + c) * width, width), width)

    def make_state(g, sub, code_ref, meta_ref):
        sums = cum_t[g]
        last = sums[rows - 1:rows, :]
        tail = jnp.exp(last - sums) * in_last
        carry = jnp.exp(last) * passes
        states = []
        for i in range(per_sub):
            c = sub * per_sub + i
            cols = columns(g, c)
            high, low = halves(v_ref[:, cols].astype(jnp.float32) * tail[:, c:c + 1])
            key = jnp.transpose(k_ref[:, cols])
            keys_turned[g * per_owner + c] = key
            states.append(jnp.dot(
                jnp.concatenate([key, key], axis=1), jnp.concatenate([high, low], axis=0),
                preferred_element_type=jnp.float32,
            ))
            meta_ref[per_sub + i:per_sub + i + 1, :] = jnp.broadcast_to(carry[:, c:c + 1], (1, width))
        for i, state in enumerate(states):
            code, scale = to_code(state)
            code_ref[i] = code
            meta_ref[i:i + 1, :] = scale

    def send_pair(sub, turn, out, into, ss, rs, m_out, m_in, m_ss, m_rs, slot, peer):
        to = place(slab, peer)
        return [
            pltpu.make_async_remote_copy(
                src_ref=m_out.at[sub, slot], dst_ref=m_in.at[sub, me], send_sem=m_ss.at[sub, turn],
                recv_sem=m_rs.at[sub, me], device_id=to, device_id_type=MESH),
            pltpu.make_async_remote_copy(
                src_ref=out.at[sub, slot], dst_ref=into.at[sub, me], send_sem=ss.at[sub, turn],
                recv_sem=rs.at[sub, me], device_id=to, device_id_type=MESH),
        ]

    def state_pair(sub, turn):
        return send_pair(sub, turn, s_out, s_in, s_ss, s_rs, sm_out, sm_in, sm_ss, sm_rs, turn, other(me, turn))

    def prefix_pair(sub, turn):
        peer = other(me, turn)
        return send_pair(sub, turn, e_out, e_in, e_ss, e_rs, em_out, em_in, em_ss, em_rs, peer, peer)

    def wait_arrival(sub, number, into, rs, m_in, m_rs):
        for ref, sem in ((m_in, m_rs), (into, rs)):
            pltpu.make_async_remote_copy(
                src_ref=ref.at[sub, number], dst_ref=ref.at[sub, number], send_sem=sem.at[sub, number],
                recv_sem=sem.at[sub, number], device_id=place(slab, number), device_id_type=MESH,
            ).wait_recv()

    def send_states(sub):
        @pl.loop(0, GROUP - 1)
        def _(step):
            turn = turn_at(step)
            make_state(other(me, turn), sub, s_out.at[sub, turn], sm_out.at[sub, turn])
            for copy in state_pair(sub, turn):
                copy.start()

        make_state(me, sub, s_in.at[sub, me], sm_in.at[sub, me])

    def near_heads(low, high):
        @pl.loop(low, high)
        def _(g):
            sums = cum_t[g]
            for batch in range(0, per_owner, BATCH):
                few = range(batch, batch + BATCH)
                scores = [
                    jnp.dot(
                        q_ref[:, columns(g, c)], keys_turned[g * per_owner + c],
                        preferred_element_type=jnp.float32,
                    )
                    for c in few
                ]
                weights = [
                    jnp.exp(
                        jnp.broadcast_to(sums[:, c:c + 1], (rows, rows))
                        - cum_rows[pl.ds(g * per_owner + c, 1), :] + bias[...]
                    )
                    for c in few
                ]
                parts = [halves(score * weight) for score, weight in zip(scores, weights)]
                results = []
                for c, (high_part, low_part) in zip(few, parts):
                    value = v_ref[:, columns(g, c)]
                    results.append(jnp.dot(
                        jnp.concatenate([high_part, low_part], axis=1),
                        jnp.concatenate([value, value], axis=0),
                        preferred_element_type=jnp.float32,
                    ))
                for c, result in zip(few, results):
                    near[:, columns(g, c)] = result

    def slab_totals(sub):
        @pl.loop(1, GROUP)
        def _(turn):
            wait_arrival(sub, other(me, turn), s_in, s_rs, sm_in, sm_rs)

        @pl.when(slab < slabs - 1)
        def _():
            @pl.loop(0, per_sub)
            def _(i):
                state = jnp.zeros((width, width), jnp.float32)
                for b in range(GROUP):
                    state = state * sm_in[sub, b, pl.ds(per_sub + i, 1), :] + from_code(s_in[sub, b, i]) * sm_in[
                        sub, b, pl.ds(i, 1), :]
                t_out[sub, i] = state

            total_copy(sub).start()

    def total_copy(sub):
        return pltpu.make_async_remote_copy(
            src_ref=t_out.at[sub], dst_ref=t_in.at[sub], send_sem=t_ss.at[sub], recv_sem=t_rs.at[sub],
            device_id=place(slab + 1, me), device_id_type=MESH)

    def send_prefixes(sub):
        @pl.when(slab > 0)
        def _():
            pltpu.make_async_remote_copy(
                src_ref=t_in.at[sub], dst_ref=t_in.at[sub], send_sem=t_ss.at[sub], recv_sem=t_rs.at[sub],
                device_id=place(slab - 1, me), device_id_type=MESH).wait_recv()

        @pl.when(slab == 0)
        def _():
            t_in[sub] = jnp.zeros(t_in.shape[1:], jnp.float32)

        @pl.loop(0, per_sub)
        def _(i):
            state = t_in[sub, i]
            for b in range(GROUP):
                code, scale = to_code(state)
                e_out[sub, b, i] = code
                em_out[sub, b, pl.ds(i, 1), :] = scale
                if b < GROUP - 1:
                    state = state * sm_in[sub, b, pl.ds(per_sub + i, 1), :] + from_code(s_in[sub, b, i]) * sm_in[
                        sub, b, pl.ds(i, 1), :]

        @pl.loop(0, GROUP - 1)
        def _(step):
            for copy in prefix_pair(sub, turn_at(step)):
                copy.start()

    def finish(g, sub, codes, metas):
        sums = cum_t[g]
        lead = jnp.exp(sums) * in_prior
        fars = []
        for i in range(per_sub):
            high, low = halves(from_code(codes[i]))
            query = q_ref[:, columns(g, sub * per_sub + i)]
            fars.append(jnp.dot(
                jnp.concatenate([query, query], axis=1), jnp.concatenate([high, low], axis=0),
                preferred_element_type=jnp.float32,
            ))
        mixes, squares = [], []
        for i, far in enumerate(fars):
            c = sub * per_sub + i
            mixed = near[:, columns(g, c)] + far * lead[:, c:c + 1] * metas[i:i + 1, :]
            mixes.append(mixed)
            squares.append(jnp.mean(mixed * mixed, axis=1, keepdims=True))
        for i, (mixed, square) in enumerate(zip(mixes, squares)):
            c = sub * per_sub + i
            gains = gain_all[pl.ds(g * per_owner + c, 1), :]
            o_ref[:, columns(g, c)] = (mixed * lax.rsqrt(square + 1e-06) * gains).astype(jnp.bfloat16)

    cum_rows = ld_all
    ld_all[...] = cum

    loads[0].wait()
    loads[1].wait()
    for sub in range(SUBS):
        send_states(sub)
    loads[2].wait()
    slab_totals(0)
    near_heads(0, 2)
    send_prefixes(0)
    near_heads(2, 3)
    slab_totals(1)
    near_heads(3, 5)
    send_prefixes(1)
    near_heads(5, GROUP)
    for sub in range(SUBS):
        finish(me, sub, e_out.at[sub, me], em_out.at[sub, me])

        @pl.loop(0, GROUP - 1)
        def _(step, sub=sub):
            g = other(me, turn_at(step))
            wait_arrival(sub, g, e_in, e_rs, em_in, em_rs)
            finish(g, sub, e_in.at[sub, g], em_in.at[sub, g])

    for sub in range(SUBS):
        @pl.loop(1, GROUP)
        def _(turn, sub=sub):
            for copy in state_pair(sub, turn) + prefix_pair(sub, turn):
                copy.wait_send()

        @pl.when(slab < slabs - 1)
        def _(sub=sub):
            total_copy(sub).wait_send()


def by_slabs(slabs, queries, keys, values, log_decay, doc_lengths, gain):
    rows, columns = queries.shape
    part = log_decay.shape[0]
    count = 2 * part
    per_sub = count // GROUP // SUBS
    width = columns // count
    codes = pltpu.VMEM((SUBS, GROUP, per_sub, width, width), jnp.int16)
    metas = pltpu.VMEM((SUBS, GROUP, 2 * per_sub, width), jnp.float32)
    totals = pltpu.VMEM((SUBS, per_sub, width, width), jnp.float32)
    sems = pltpu.SemaphoreType.DMA
    vmem = pl.BlockSpec(memory_space=pltpu.VMEM)
    return pl.pallas_call(
        functools.partial(slab_kernel, slabs),
        out_shape=jax.ShapeDtypeStruct((rows, columns), jnp.bfloat16),
        in_specs=[pl.BlockSpec(memory_space=pltpu.SMEM)] + [pl.BlockSpec(memory_space=pltpu.HBM)] * 3 + [vmem] * 2,
        out_specs=vmem,
        scratch_shapes=[pltpu.VMEM((rows, columns), jnp.bfloat16)] * 3 + [
            pltpu.VMEM((count, width, rows), jnp.bfloat16),
            pltpu.VMEM((count, rows), jnp.float32),
            pltpu.VMEM((count, width), jnp.float32),
            pltpu.VMEM((GROUP, rows, count // GROUP), jnp.float32),
            pltpu.VMEM((rows, rows), jnp.float32),
            pltpu.VMEM((rows, columns), jnp.float32),
            codes, codes, metas, metas, codes, codes, metas, metas, totals, totals,
        ] + [sems((SUBS, GROUP))] * 8 + [sems((SUBS,))] * 2 + [sems((2,))] * 2 + [sems((3,))],
        compiler_params=pltpu.CompilerParams(
            collective_id=0, has_side_effects=True, vmem_limit_bytes=50 * 1024 * 1024
        ),
        cost_estimate=pl.CostEstimate(
            flops=14 * count * rows * rows * width, bytes_accessed=8 * rows * columns,
            transcendentals=count * rows * rows,
        ),
    )(doc_lengths, queries, keys, values, log_decay, gain.reshape(part, width))


def solution(mesh):
    devices = mesh.shape["seq"] * mesh.shape["head"]

    def run(queries, keys, values, log_decay, doc_lengths, gain):
        rows = queries.shape[0] // devices
        heads = log_decay.shape[0]
        width = queries.shape[1] // heads
        fits = (
            mesh.shape["head"] == 2 and devices % GROUP == 0 and rows == width == 128
            and GROUP * rows * 4 >= queries.shape[0] and heads % (GROUP * SUBS) == 0 and heads <= rows
        )
        body = functools.partial(by_slabs, devices // GROUP) if fits else local
        return jax.shard_map(
            body,
            mesh=mesh,
            in_specs=(
                P(("seq", "head"), None),
                P(("seq", "head"), None),
                P(("seq", "head"), None),
                P("head", "seq"),
                P(),
                P("head"),
            ),
            out_specs=P(("seq", "head"), None),
            check_vma=False,
        )(queries, keys, values, log_decay, doc_lengths, gain)

    return run
```

```python
import functools

import jax
import jax.numpy as jnp
from jax import lax
from jax.experimental import pallas as pl
from jax.experimental.pallas import tpu as pltpu
from jax.sharding import PartitionSpec as P

HIGHEST = lax.Precision.HIGHEST


def prefix(part, axis, combine, identity):
    place = lax.axis_index(axis)
    gathered = jax.tree.map(lambda a: lax.all_gather(a, axis), part)
    state = jax.tree.map(lambda a, e: jnp.zeros_like(a) + jnp.asarray(e, a.dtype), part, identity)

    def one(turn, state):
        return combine(
            state, jax.tree.map(lambda a: lax.dynamic_index_in_dim(a, turn, 0, False), gathered)
        )

    return lax.fori_loop(0, place, one, state)


def link(earlier, later):
    factor_one, state_one = earlier
    factor_two, state_two = later
    return (factor_one * factor_two, factor_two[:, None, None] * state_one + state_two)


def make_identity(amount, head_width):
    return (
        jnp.ones((amount,), jnp.float32),
        jnp.zeros((amount, head_width, head_width), jnp.float32),
    )


def local(queries, keys, values, log_decay, doc_lengths, gain):
    query_rows, key_rows, value_rows = (
        lax.all_to_all(queries, "head", split_axis=1, concat_axis=0, tiled=True),
        lax.all_to_all(keys, "head", split_axis=1, concat_axis=0, tiled=True),
        lax.all_to_all(values, "head", split_axis=1, concat_axis=0, tiled=True),
    )
    head_count = log_decay.shape[0]
    row_count = key_rows.shape[0]
    head_width = key_rows.shape[1] // head_count
    doc_ends = jnp.cumsum(doc_lengths)
    first_row = lax.axis_index("seq") * row_count
    positions = first_row + jnp.arange(row_count, dtype=jnp.int32)
    doc_ids = jnp.sum((doc_ends[None, :] <= positions[:, None]).astype(jnp.int32), axis=1)
    prior_doc = jnp.sum((doc_ends <= first_row - 1).astype(jnp.int32))
    order_ids = jnp.arange(row_count, dtype=jnp.int32)
    allowed = (order_ids[:, None] >= order_ids[None, :]) & (doc_ids[:, None] == doc_ids[None, :])
    decay_sum = jnp.cumsum(log_decay, axis=1)
    tailing = (
        jnp.exp(decay_sum[:, -1:] - decay_sum)
        * (doc_ids == doc_ids[-1]).astype(jnp.float32)[None, :]
    )
    leading = jnp.exp(decay_sum) * (doc_ids == prior_doc).astype(jnp.float32)[None, :]
    carried = jnp.exp(decay_sum[:, -1]) * (doc_ids[-1] == prior_doc).astype(jnp.float32)
    head_ids = jnp.arange(head_count, dtype=jnp.int32)

    def pick(block, head_index):
        return lax.dynamic_slice_in_dim(block, head_index * head_width, head_width, 1)

    def own_state(head_index):
        weighted = pick(key_rows, head_index).astype(jnp.float32) * tailing[head_index][:, None]
        value_part = pick(value_rows, head_index).astype(jnp.float32)
        return jnp.einsum(
            "jd,je->de", weighted, value_part, precision=HIGHEST, preferred_element_type=jnp.float32
        )

    def within(head_index):
        scores = lax.dot_general(
            pick(query_rows, head_index),
            pick(key_rows, head_index),
            (((1,), (1,)), ((), ())),
            preferred_element_type=jnp.float32,
        )
        gaps = decay_sum[head_index][:, None] - decay_sum[head_index][None, :]
        weights = jnp.where(allowed, jnp.exp(jnp.where(allowed, gaps, 0.0)), 0.0)
        value_part = pick(value_rows, head_index).astype(jnp.float32)
        return jnp.dot(
            scores * weights, value_part, precision=HIGHEST, preferred_element_type=jnp.float32
        )

    def across(paired):
        head_index, state = paired
        scaled = pick(query_rows, head_index).astype(jnp.float32) * leading[head_index][:, None]
        return jnp.dot(scaled, state, precision=HIGHEST, preferred_element_type=jnp.float32)

    own = lax.map(own_state, head_ids)
    total_factor, incoming = prefix(
        (carried, own), "seq", link, make_identity(head_count, head_width)
    )
    far = lax.map(across, (head_ids, incoming))
    near = lax.map(within, head_ids)
    mixed = near + far
    mean_square = jnp.mean(mixed * mixed, axis=-1, keepdims=True)
    normed = mixed * lax.rsqrt(mean_square + 1e-06) * gain.reshape(head_count, 1, head_width)
    merged = (
        jnp.transpose(normed, (1, 0, 2))
        .reshape(row_count, head_count * head_width)
        .astype(jnp.bfloat16)
    )
    return lax.all_to_all(merged, "head", split_axis=0, concat_axis=1, tiled=True)


MESH = pl.DeviceIdType.MESH
GROUP = 8
SUBS = 2
BATCH = 4
TOP = 32766.0
NEAREST = 12582912.0
FAR_BELOW = -1e30
ORDER = (7, 6, 1, 5, 4, 3, 2)


def other(number, turn):
    out = 0
    for bit in (1, 2, 4):
        a, b = (number // bit) % 2, (turn // bit) % 2
        out = out + bit * (a + b - 2 * a * b)
    return out


def turn_at(step):
    out = 0
    for i, turn in enumerate(ORDER):
        out = out + jnp.where(step == i, turn, 0)
    return out


def halves(x):
    high = x.astype(jnp.bfloat16)
    return high, (x - high.astype(jnp.float32)).astype(jnp.bfloat16)


def to_code(state):
    scale = jnp.maximum(jnp.max(jnp.abs(state), axis=0, keepdims=True), 1e-30) * (1.0 / TOP)
    code = (state * (1.0 / scale) + NEAREST - NEAREST).astype(jnp.int32).astype(jnp.int16)
    return code, scale


def from_code(code):
    return code.astype(jnp.int32).astype(jnp.float32)


def slab_kernel(
    slabs,
    doc_ref, q_far, k_far, v_far, ld_ref, gain_ref, o_ref,
    q_ref, k_ref, v_ref, keys_turned,
    ld_all, gain_all, cum_t, bias, near,
    s_out, s_in, sm_out, sm_in, e_out, e_in, em_out, em_in, t_out, t_in,
    s_ss, s_rs, sm_ss, sm_rs, e_ss, e_rs, em_ss, em_rs, t_ss, t_rs, x_ss, x_rs, l_s,
):
    seq, half = lax.axis_index("seq"), lax.axis_index("head")
    block = seq * 2 + half
    slab, me = block // GROUP, block % GROUP
    rows, width = q_ref.shape[0], q_ref.shape[0]
    part = ld_ref.shape[0]
    count = 2 * part
    per_owner = count // GROUP
    per_sub = per_owner // SUBS

    def place(other_slab, number):
        b = other_slab * GROUP + number
        return (b // 2, b % 2)

    loads = [
        pltpu.make_async_copy(far_ref, near_ref, l_s.at[i])
        for i, (far_ref, near_ref) in enumerate(((k_far, k_ref), (v_far, v_ref), (q_far, q_ref)))
    ]
    for load in loads:
        load.start()

    barrier = pltpu.get_barrier_semaphore()
    for turn in range(1, GROUP):
        pl.semaphore_signal(barrier, inc=1, device_id=place(slab, other(me, turn)), device_id_type=MESH)

    @pl.when(slab > 0)
    def _():
        pl.semaphore_signal(barrier, inc=1, device_id=place(slab - 1, me), device_id_type=MESH)

    @pl.when(slab < slabs - 1)
    def _():
        pl.semaphore_signal(barrier, inc=1, device_id=place(slab + 1, me), device_id_type=MESH)

    neighbours = GROUP - 1 + jnp.where(slab > 0, 1, 0) + jnp.where(slab < slabs - 1, 1, 0)
    pl.semaphore_wait(barrier, neighbours)

    mine = pl.ds(pl.multiple_of(half * part, part), part)
    swaps = [
        pltpu.make_async_remote_copy(
            src_ref=ld_ref.at[:, pl.ds(pl.multiple_of((1 - half) * rows, rows), rows)],
            dst_ref=ld_all.at[mine], send_sem=x_ss.at[0], recv_sem=x_rs.at[0],
            device_id=(seq, 1 - half), device_id_type=MESH),
        pltpu.make_async_remote_copy(
            src_ref=gain_ref, dst_ref=gain_all.at[mine], send_sem=x_ss.at[1], recv_sem=x_rs.at[1],
            device_id=(seq, 1 - half), device_id_type=MESH),
    ]
    for swap in swaps:
        swap.start()
    keeps = [
        pltpu.make_async_copy(
            ld_ref.at[:, pl.ds(pl.multiple_of(half * rows, rows), rows)], ld_all.at[mine], l_s.at[3]),
        pltpu.make_async_copy(gain_ref, gain_all.at[mine], l_s.at[4]),
    ]
    for keep in keeps:
        keep.start()

    first = block * rows
    down = lax.broadcasted_iota(jnp.int32, (rows, rows), 0)
    along = lax.broadcasted_iota(jnp.int32, (rows, rows), 1)
    doc_down = jnp.zeros((rows, rows), jnp.int32)
    doc_along = jnp.zeros((rows, rows), jnp.int32)
    prior = jnp.int32(0)
    final = jnp.int32(0)
    end = jnp.int32(0)
    for n in range(doc_ref.shape[0]):
        end = end + doc_ref[n]
        doc_down = doc_down + (down + first >= end).astype(jnp.int32)
        doc_along = doc_along + (along + first >= end).astype(jnp.int32)
        prior = prior + (end <= first - 1).astype(jnp.int32)
        final = final + (end <= first + rows - 1).astype(jnp.int32)
    bias[...] = jnp.where((down >= along) & (doc_down == doc_along), 0.0, FAR_BELOW)
    doc_few = doc_down[:, :per_owner]
    in_last = (doc_few == final).astype(jnp.float32)
    in_prior = (doc_few == prior).astype(jnp.float32)
    passes = (jnp.full((1, per_owner), final, jnp.int32) == prior).astype(jnp.float32)

    for copy in keeps + swaps:
        copy.wait()
    cum = jnp.dot(
        ld_all[...], (down <= along).astype(jnp.float32),
        precision=HIGHEST, preferred_element_type=jnp.float32,
    )
    turned = jnp.transpose(jnp.concatenate([cum, jnp.zeros((rows - count, rows), jnp.float32)], axis=0))
    for g in range(GROUP):
        cum_t[g] = turned[:, g * per_owner:(g + 1) * per_owner]

    def columns(g, c):
        return pl.ds(pl.multiple_of((g * per_owner + c) * width, width), width)

    def make_state(g, sub, code_ref, meta_ref):
        sums = cum_t[g]
        last = sums[rows - 1:rows, :]
        tail = jnp.exp(last - sums) * in_last
        carry = jnp.exp(last) * passes
        states = []
        for i in range(per_sub):
            c = sub * per_sub + i
            cols = columns(g, c)
            high, low = halves(v_ref[:, cols].astype(jnp.float32) * tail[:, c:c + 1])
            key = jnp.transpose(k_ref[:, cols])
            keys_turned[g * per_owner + c] = key
            states.append(jnp.dot(
                jnp.concatenate([key, key], axis=1), jnp.concatenate([high, low], axis=0),
                preferred_element_type=jnp.float32,
            ))
            meta_ref[per_sub + i:per_sub + i + 1, :] = jnp.broadcast_to(carry[:, c:c + 1], (1, width))
        for i, state in enumerate(states):
            code, scale = to_code(state)
            code_ref[i] = code
            meta_ref[i:i + 1, :] = scale

    def send_pair(sub, turn, out, into, ss, rs, m_out, m_in, m_ss, m_rs, slot, peer):
        to = place(slab, peer)
        return [
            pltpu.make_async_remote_copy(
                src_ref=m_out.at[sub, slot], dst_ref=m_in.at[sub, me], send_sem=m_ss.at[sub, turn],
                recv_sem=m_rs.at[sub, me], device_id=to, device_id_type=MESH),
            pltpu.make_async_remote_copy(
                src_ref=out.at[sub, slot], dst_ref=into.at[sub, me], send_sem=ss.at[sub, turn],
                recv_sem=rs.at[sub, me], device_id=to, device_id_type=MESH),
        ]

    def state_pair(sub, turn):
        return send_pair(sub, turn, s_out, s_in, s_ss, s_rs, sm_out, sm_in, sm_ss, sm_rs, turn, other(me, turn))

    def prefix_pair(sub, turn):
        peer = other(me, turn)
        return send_pair(sub, turn, e_out, e_in, e_ss, e_rs, em_out, em_in, em_ss, em_rs, peer, peer)

    def wait_arrival(sub, number, into, rs, m_in, m_rs):
        for ref, sem in ((m_in, m_rs), (into, rs)):
            pltpu.make_async_remote_copy(
                src_ref=ref.at[sub, number], dst_ref=ref.at[sub, number], send_sem=sem.at[sub, number],
                recv_sem=sem.at[sub, number], device_id=place(slab, number), device_id_type=MESH,
            ).wait_recv()

    def send_states(sub):
        @pl.loop(0, GROUP - 1)
        def _(step):
            turn = turn_at(step)
            make_state(other(me, turn), sub, s_out.at[sub, turn], sm_out.at[sub, turn])
            for copy in state_pair(sub, turn):
                copy.start()

        make_state(me, sub, s_in.at[sub, me], sm_in.at[sub, me])

    def near_heads(low, high):
        @pl.loop(low, high)
        def _(g):
            sums = cum_t[g]
            for batch in range(0, per_owner, BATCH):
                few = range(batch, batch + BATCH)
                scores = [
                    jnp.dot(
                        q_ref[:, columns(g, c)], keys_turned[g * per_owner + c],
                        preferred_element_type=jnp.float32,
                    )
                    for c in few
                ]
                weights = [
                    jnp.exp(
                        jnp.broadcast_to(sums[:, c:c + 1], (rows, rows))
                        - cum_rows[pl.ds(g * per_owner + c, 1), :] + bias[...]
                    )
                    for c in few
                ]
                parts = [halves(score * weight) for score, weight in zip(scores, weights)]
                results = []
                for c, (high_part, low_part) in zip(few, parts):
                    value = v_ref[:, columns(g, c)]
                    results.append(jnp.dot(
                        jnp.concatenate([high_part, low_part], axis=1),
                        jnp.concatenate([value, value], axis=0),
                        preferred_element_type=jnp.float32,
                    ))
                for c, result in zip(few, results):
                    near[:, columns(g, c)] = result

    def slab_totals(sub):
        @pl.loop(1, GROUP)
        def _(turn):
            wait_arrival(sub, other(me, turn), s_in, s_rs, sm_in, sm_rs)

        @pl.when(slab < slabs - 1)
        def _():
            @pl.loop(0, per_sub)
            def _(i):
                state = jnp.zeros((width, width), jnp.float32)
                for b in range(GROUP):
                    state = state * sm_in[sub, b, pl.ds(per_sub + i, 1), :] + from_code(s_in[sub, b, i]) * sm_in[
                        sub, b, pl.ds(i, 1), :]
                t_out[sub, i] = state

            total_copy(sub).start()

    def total_copy(sub):
        return pltpu.make_async_remote_copy(
            src_ref=t_out.at[sub], dst_ref=t_in.at[sub], send_sem=t_ss.at[sub], recv_sem=t_rs.at[sub],
            device_id=place(slab + 1, me), device_id_type=MESH)

    def send_prefixes(sub):
        @pl.when(slab > 0)
        def _():
            pltpu.make_async_remote_copy(
                src_ref=t_in.at[sub], dst_ref=t_in.at[sub], send_sem=t_ss.at[sub], recv_sem=t_rs.at[sub],
                device_id=place(slab - 1, me), device_id_type=MESH).wait_recv()

        @pl.when(slab == 0)
        def _():
            t_in[sub] = jnp.zeros(t_in.shape[1:], jnp.float32)

        @pl.loop(0, per_sub)
        def _(i):
            state = t_in[sub, i]
            for b in range(GROUP):
                code, scale = to_code(state)
                e_out[sub, b, i] = code
                em_out[sub, b, pl.ds(i, 1), :] = scale
                if b < GROUP - 1:
                    state = state * sm_in[sub, b, pl.ds(per_sub + i, 1), :] + from_code(s_in[sub, b, i]) * sm_in[
                        sub, b, pl.ds(i, 1), :]

        @pl.loop(0, GROUP - 1)
        def _(step):
            for copy in prefix_pair(sub, turn_at(step)):
                copy.start()

    def finish(g, sub, codes, metas):
        sums = cum_t[g]
        lead = jnp.exp(sums) * in_prior
        fars = []
        for i in range(per_sub):
            high, low = halves(from_code(codes[i]))
            query = q_ref[:, columns(g, sub * per_sub + i)]
            fars.append(jnp.dot(
                jnp.concatenate([query, query], axis=1), jnp.concatenate([high, low], axis=0),
                preferred_element_type=jnp.float32,
            ))
        mixes, squares = [], []
        for i, far in enumerate(fars):
            c = sub * per_sub + i
            mixed = near[:, columns(g, c)] + far * lead[:, c:c + 1] * metas[i:i + 1, :]
            mixes.append(mixed)
            squares.append(jnp.mean(mixed * mixed, axis=1, keepdims=True))
        for i, (mixed, square) in enumerate(zip(mixes, squares)):
            c = sub * per_sub + i
            gains = gain_all[pl.ds(g * per_owner + c, 1), :]
            o_ref[:, columns(g, c)] = (mixed * lax.rsqrt(square + 1e-06) * gains).astype(jnp.bfloat16)

    cum_rows = ld_all
    ld_all[...] = cum

    loads[0].wait()
    loads[1].wait()
    for sub in range(SUBS):
        send_states(sub)
    loads[2].wait()
    slab_totals(0)
    near_heads(0, 2)
    send_prefixes(0)
    near_heads(2, 3)
    slab_totals(1)
    near_heads(3, 5)
    send_prefixes(1)
    near_heads(5, GROUP)
    for sub in range(SUBS):
        finish(me, sub, e_out.at[sub, me], em_out.at[sub, me])

        @pl.loop(0, GROUP - 1)
        def _(step, sub=sub):
            g = other(me, turn_at(step))
            wait_arrival(sub, g, e_in, e_rs, em_in, em_rs)
            finish(g, sub, e_in.at[sub, g], em_in.at[sub, g])

    for sub in range(SUBS):
        @pl.loop(1, GROUP)
        def _(turn, sub=sub):
            for copy in state_pair(sub, turn) + prefix_pair(sub, turn):
                copy.wait_send()

        @pl.when(slab < slabs - 1)
        def _(sub=sub):
            total_copy(sub).wait_send()


def by_slabs(slabs, queries, keys, values, log_decay, doc_lengths, gain):
    rows, columns = queries.shape
    part = log_decay.shape[0]
    count = 2 * part
    per_sub = count // GROUP // SUBS
    width = columns // count
    codes = pltpu.VMEM((SUBS, GROUP, per_sub, width, width), jnp.int16)
    metas = pltpu.VMEM((SUBS, GROUP, 2 * per_sub, width), jnp.float32)
    totals = pltpu.VMEM((SUBS, per_sub, width, width), jnp.float32)
    sems = pltpu.SemaphoreType.DMA
    vmem = pl.BlockSpec(memory_space=pltpu.VMEM)
    return pl.pallas_call(
        functools.partial(slab_kernel, slabs),
        out_shape=jax.ShapeDtypeStruct((rows, columns), jnp.bfloat16),
        in_specs=[pl.BlockSpec(memory_space=pltpu.SMEM)] + [pl.BlockSpec(memory_space=pltpu.HBM)] * 5,
        out_specs=vmem,
        scratch_shapes=[pltpu.VMEM((rows, columns), jnp.bfloat16)] * 3 + [
            pltpu.VMEM((count, width, rows), jnp.bfloat16),
            pltpu.VMEM((count, rows), jnp.float32),
            pltpu.VMEM((count, width), jnp.float32),
            pltpu.VMEM((GROUP, rows, count // GROUP), jnp.float32),
            pltpu.VMEM((rows, rows), jnp.float32),
            pltpu.VMEM((rows, columns), jnp.float32),
            codes, codes, metas, metas, codes, codes, metas, metas, totals, totals,
        ] + [sems((SUBS, GROUP))] * 8 + [sems((SUBS,))] * 2 + [sems((2,))] * 2 + [sems((5,))],
        compiler_params=pltpu.CompilerParams(
            collective_id=0, has_side_effects=True, vmem_limit_bytes=50 * 1024 * 1024
        ),
        cost_estimate=pl.CostEstimate(
            flops=14 * count * rows * rows * width, bytes_accessed=8 * rows * columns,
            transcendentals=count * rows * rows,
        ),
    )(doc_lengths, queries, keys, values, log_decay, gain.reshape(part, width))


def solution(mesh):
    devices = mesh.shape["seq"] * mesh.shape["head"]

    def run(queries, keys, values, log_decay, doc_lengths, gain):
        rows = queries.shape[0] // devices
        heads = log_decay.shape[0]
        width = queries.shape[1] // heads
        fits = (
            mesh.shape["head"] == 2 and devices % GROUP == 0 and rows == width == 128
            and GROUP * rows * 4 >= queries.shape[0] and heads % (GROUP * SUBS) == 0 and heads <= rows
        )
        body = functools.partial(by_slabs, devices // GROUP) if fits else local
        return jax.shard_map(
            body,
            mesh=mesh,
            in_specs=(
                P(("seq", "head"), None),
                P(("seq", "head"), None),
                P(("seq", "head"), None),
                P("head", "seq"),
                P(),
                P("head"),
            ),
            out_specs=P(("seq", "head"), None),
            check_vma=False,
        )(queries, keys, values, log_decay, doc_lengths, gain)

    return run
```
